512 devices in a mesh: seq: 64 (over z, x), head: 8 (over y, core).
Axes of the slice: x: 4, y: 4, z: 16, core: 2. Of those that a mesh axis runs over, the one named last changes fastest.
Arguments:
- query_input: bfloat16 [8192, 5120], P(('seq', 'head')), may hold values from -6 to 6
- key_input: bfloat16 [32768, 5120], P(('seq', 'head')), may hold values from -6 to 6
- value_input: bfloat16 [32768, 5120], P(('seq', 'head')), may hold values from -6 to 6
- query_gain: float32 [5120], replicated, may hold values from 0.1 to 1.9
- key_gain: float32 [5120], replicated, may hold values from 0.1 to 1.9
- band_lists: int32 [64, 8], replicated, may hold values from -1 to 255, as said below
- out_weight: bfloat16 [5120, 5120], P('head', 'seq'), may hold values from -4 to 4
Outputs:
- projected: bfloat16 [8192, 5120], P('seq', 'head')
The draws below stay inside these ranges and needn't reach their ends.
Inputs may be any that keep to these rules, and one draw needn't show every extreme that they name: `band_lists`: each row lists distinct key blocks, live entries first and then -1, 3 or more live. Entry 0 of query block j is key block 4 * j. Every listed block b has |b // 4 - j| <= 2; for query block j, at most 2 distinct blocks are listed from each of s - 1 and s + 1 and at most 1 from each of s - 2 and s + 2, and these counts are reached wherever that index exists.
All inputs are finite; a program needn't handle non-finite values.
Results may differ from the reference program's by a relative error of at most 0.017.
The reference program's roundings to bfloat16 on the way count: a program that leaves them out, or rounds other values in their place, can miss the bound.
Values may be sent and summed in bfloat16 or wider, within the bound.
No kernel may reach another device: no remote copies, remote signals or barrier semaphores. Data moves between devices by JAX's collectives and lax.ppermute only.
A program may use at most 64 MiB of HBM per device.

```python
import jax
import jax.numpy as jnp
from jax import lax

D = 5120
HEADS = 40
HD = 128
BT = 128
QB_DEV = 1
KB_DEV = 4
MAXB = 8
NEAR = 2
FAR = 1
QBLOCKS = 64
KBLOCKS = 256
N_SEQ = 64
N_HEAD = 8


def draw_query_input(key, part):
    key = jax.random.fold_in(key, 1)
    array_shape = (QBLOCKS, BT, HEADS, HD)
    result_array = jnp.clip(jax.random.normal(key, array_shape, jnp.float32), -6.0, 6.0)
    return result_array.reshape(QBLOCKS * BT, HEADS * HD).astype(jnp.bfloat16)


def draw_key_input(key, part):
    key = jax.random.fold_in(key, 2)
    array_shape = (KBLOCKS, BT, HEADS, HD)
    result_array = jnp.clip(jax.random.normal(key, array_shape, jnp.float32), -6.0, 6.0)
    return result_array.reshape(KBLOCKS * BT, HEADS * HD).astype(jnp.bfloat16)


def draw_band_lists(key, part):
    key = jax.random.fold_in(key, 3)
    first_key, second_key, third_key = jax.random.split(key, 3)
    side_scores = jax.random.randint(first_key, (N_SEQ, 4, KB_DEV), 0, 1 << 20) * KB_DEV + jnp.arange(KB_DEV)
    orders = jnp.argsort(side_scores, axis=-1).astype(jnp.int32)
    devices = jnp.arange(N_SEQ, dtype=jnp.int32)[:, None]
    option_device = jnp.concatenate([jnp.broadcast_to(devices, (N_SEQ, KB_DEV)), jnp.broadcast_to(devices - 2, (N_SEQ, FAR)), jnp.broadcast_to(devices - 1, (N_SEQ, NEAR)), jnp.broadcast_to(devices + 1, (N_SEQ, NEAR)), jnp.broadcast_to(devices + 2, (N_SEQ, FAR))], axis=1)
    option_block = jnp.concatenate([jnp.broadcast_to(jnp.arange(KB_DEV, dtype=jnp.int32)[None, :], (N_SEQ, KB_DEV)), orders[:, 0, :FAR], orders[:, 1, :NEAR], orders[:, 2, :NEAR], orders[:, 3, :FAR]], axis=1)
    option_valid = (option_device >= 0) & (option_device < N_SEQ)
    option_ids = option_device * KB_DEV + option_block
    option_count = KB_DEV + 2 * NEAR + 2 * FAR
    block_index = jnp.arange(QBLOCKS, dtype=jnp.int32)
    owner_index = block_index // QB_DEV
    local_index = block_index % QB_DEV
    row_ids = option_ids[owner_index]
    row_valid = option_valid[owner_index]
    column = jnp.arange(option_count, dtype=jnp.int32)[None, :]
    diagonal = column == (local_index % KB_DEV)[:, None]
    forced = (local_index == 0)[:, None] & (column >= KB_DEV) & row_valid
    priority = jax.random.randint(second_key, (QBLOCKS, option_count), 0, 1 << 20) * option_count + column
    ranking = jnp.where(diagonal, -2, jnp.where(forced, -1, jnp.where(row_valid, priority, (1 << 30) + column)))
    sorted_order = jnp.argsort(ranking, axis=1)[:, :MAXB]
    picked = jnp.take_along_axis(row_ids, sorted_order, axis=1)
    live_count = jax.random.randint(third_key, (QBLOCKS,), 3, MAXB + 1)
    lowest = 1 + jnp.sum(forced.astype(jnp.int32), axis=1)
    highest = jnp.minimum(jnp.sum(row_valid.astype(jnp.int32), axis=1), MAXB)
    live_count = jnp.minimum(jnp.maximum(live_count, lowest), highest)
    return jnp.where(jnp.arange(MAXB)[None, :] < live_count[:, None], picked, -1).astype(jnp.int32)


def with_spikes(entries, rng, source, target, shards_of, factor):
    def block_of(dim):
        return (jnp.arange(entries.shape[dim]) // (entries.shape[dim] // shards_of)).reshape((-1,) + (1,) * (entries.ndim - 1 - dim))

    first = jax.random.permutation(rng, shards_of)[block_of(target)]
    other_side = (block_of(target) + shards_of // 2) % shards_of
    return jnp.where((block_of(source) == first) | (block_of(source) == other_side), factor * entries, entries)


def block_scale(own_key, shape, cuts, low, high):
    level, own = 1.0, jax.random.fold_in(own_key, 6)
    for axis_at, shards_of in cuts:
        draws = jnp.exp(jax.random.uniform(jax.random.fold_in(own, axis_at), (shards_of,), jnp.float32, low / len(cuts), high / len(cuts)))
        level = level * jnp.repeat(draws, shape[axis_at] // shards_of).reshape([-1 if axis == axis_at else 1 for axis in range(len(shape))])
    return level


def centred(own_key, dims, width, most, cuts=(), held_as=jnp.bfloat16):
    values = width * jax.random.normal(own_key, dims, jnp.float32)
    if cuts:
        values = values * block_scale(own_key, dims, cuts, -0.22, 0.18)
    return jnp.clip(values, -most, most).astype(held_as)


def noise_with(own_key, shape, spread, reach, shards, heavy, kind=jnp.bfloat16):
    values = spread * jax.random.normal(own_key, shape, jnp.float32)
    if shards:
        values = values * block_scale(own_key, shape, shards, -0.22, 0.18)
    return jnp.clip(with_spikes(values, jax.random.fold_in(own_key, 3), *heavy), -reach, reach).astype(kind)


def setup_inputs(seed: int = 0) -> dict:
    arg_keys = jax.random.split(jax.random.key(seed), 8)
    return {
        "query_input": draw_query_input(jax.random.fold_in(arg_keys[7], 71), 0),
        "key_input": draw_key_input(jax.random.fold_in(arg_keys[7], 71), 0),
        "value_input": centred(arg_keys[2], (KBLOCKS * BT, D), 1.0, 6.0, ((0, 512),)),
        "query_gain": jnp.clip(1.0 + 0.18 * jax.random.normal(arg_keys[3], (D,), jnp.float32), 0.1, 1.9),
        "key_gain": jnp.clip(1.0 + 0.18 * jax.random.normal(arg_keys[4], (D,), jnp.float32), 0.1, 1.9),
        "band_lists": draw_band_lists(jax.random.fold_in(arg_keys[7], 71), 0),
        "out_weight": noise_with(arg_keys[6], (D, D), 16 ** -0.5, 4.0, ((0, 8), (1, 64)), (0, 1, 64, 4.0)),
    }


def normalize(band_rows, gain_vector):
    widened = band_rows.astype(jnp.float32)
    inverse = lax.rsqrt(lax.optimization_barrier(jnp.mean(widened * widened, axis=-1, keepdims=True)) + 1e-06)
    return (widened * inverse * gain_vector).astype(jnp.bfloat16)

def reference(query_input, key_input, value_input, query_gain, key_gain, band_lists, out_weight):
    query_blocks = normalize(query_input, query_gain).reshape(QBLOCKS, BT, HEADS, HD)
    key_blocks = normalize(key_input, key_gain).reshape(KBLOCKS, BT, HEADS, HD)
    value_blocks = value_input.reshape(KBLOCKS, BT, HEADS, HD)

    def attend(inputs):
        query_tile, listing = inputs
        listed = listing >= 0
        safe_ids = jnp.maximum(listing, 0).astype(jnp.int32)
        key_tiles = key_blocks[safe_ids].astype(jnp.float32)
        value_tiles = value_blocks[safe_ids].astype(jnp.float32)
        scores = jnp.einsum('qhd,mkhd->hqmk', query_tile.astype(jnp.float32), key_tiles) * HD ** (-0.5)
        scores = jnp.where(listed[None, None, :, None], scores, -jnp.inf)
        row_max = lax.optimization_barrier(jnp.max(scores, axis=(2, 3), keepdims=True))
        exponent = jnp.exp(scores - row_max)
        totals = lax.optimization_barrier(jnp.sum(exponent, axis=(2, 3)))
        weights = lax.optimization_barrier(exponent.astype(jnp.bfloat16)).astype(jnp.float32)
        attended = jnp.einsum('hqmk,mkhd->qhd', weights, value_tiles) / jnp.transpose(totals)[:, :, None]
        return attended.astype(jnp.bfloat16).reshape(BT, HEADS * HD)
    attended = lax.map(attend, (query_blocks, band_lists)).reshape(QBLOCKS * BT, HEADS * HD)
    group_width = HEADS * HD // N_HEAD
    by_group = jnp.transpose(attended.reshape(QBLOCKS * BT, N_HEAD, group_width), (1, 0, 2))
    weight_groups = out_weight.reshape(N_HEAD, group_width, D)

    def accumulate(running, operands):
        partial_value = jnp.dot(operands[0], operands[1], preferred_element_type=jnp.float32)
        rounded = lax.optimization_barrier(partial_value.astype(jnp.bfloat16))
        return (running + rounded.astype(jnp.float32), None)
    summed, unused = lax.scan(accumulate, jnp.zeros((QBLOCKS * BT, D), jnp.float32), (by_group, weight_groups))
    return summed.astype(jnp.bfloat16)
```

```python
import jax
import jax.numpy as jnp
from jax import lax
from jax.experimental import pallas as pl
from jax.experimental.pallas import tpu as pltpu
from jax.sharding import Mesh, PartitionSpec as P

HD = 128
HALF = 64
QROWS = 16
NX = 4
NH = 8
NZ = 16
MAXB = 8
GROUP = 5
K0, V0, K5, V5, Q0, Q5, CHUNK = 0, 64, 128, 144, 160, 176, 192
KV = 160
BF = jnp.bfloat16
F32 = jnp.float32
VMEM = pl.BlockSpec(memory_space=pltpu.VMEM)
SMEM = pl.BlockSpec(memory_space=pltpu.SMEM)
ANY = pl.BlockSpec(memory_space=pl.ANY)
LIMIT = 40 * 1024 * 1024


def dot(a, b, contract):
    return lax.dot_general(a, b, ((contract[:1], contract[1:]), ((), ())), preferred_element_type=F32)


def pack_kernel(q_ref, k_ref, v_ref, qg_ref, kg_ref, out_ref):
    def inverse(ref):
        wide = ref[...].astype(F32)
        return lax.rsqrt(jnp.mean(wide * wide, axis=-1, keepdims=True) + 1e-06)

    q_inv, k_inv = inverse(q_ref), inverse(k_ref)
    for group in range(NH):
        for at in range(GROUP):
            cols = slice((group * GROUP + at) * HD, (group * GROUP + at + 1) * HD)
            q = (q_ref[:, cols].astype(F32) * q_inv * qg_ref[:, cols]).astype(BF)
            k = (k_ref[:, cols].astype(F32) * k_inv * kg_ref[:, cols]).astype(BF)
            v = v_ref[:, cols]
            if at < NX:
                chunk = at * NH + group
                out_ref[chunk, K0 : K0 + HALF] = k
                out_ref[chunk, V0 : V0 + HALF] = v
                out_ref[chunk, Q0 : Q0 + QROWS] = q
            else:
                for x in range(NX):
                    chunk = x * NH + group
                    rows = slice(x * 16, x * 16 + 16)
                    out_ref[chunk, K5 : K5 + 16] = k[rows]
                    out_ref[chunk, V5 : V5 + 16] = v[rows]
                    out_ref[chunk, Q5 : Q5 + QROWS] = q


def listed_of(lists, block, seq, count):
    found = [jnp.int32(-1)] * count
    for m in range(MAXB):
        entry = lists[block * MAXB + m]
        hit = (entry >= 0) & ((entry >> 2) == seq)
        for i in reversed(range(count)):
            free = found[i] < 0
            if i:
                free = free & (found[i - 1] >= 0)
            found[i] = jnp.where(hit & free, entry, found[i])
    return found


def select_kernel(lists, zi, r_ref, up_ref, down_ref, sems):
    z = zi[0]
    above = jnp.minimum(z + 1, NZ - 1) * 4
    below = jnp.maximum(z - 1, 0) * 4
    first = z * 4
    up = (
        listed_of(lists, above, first + 2, 1)
        + listed_of(lists, above, first + 3, 2)
        + listed_of(lists, above + 1, first + 3, 1)
    )
    down = (
        listed_of(lists, below + 3, first + 1, 1)
        + listed_of(lists, below + 3, first, 2)
        + listed_of(lists, below + 2, first, 1)
    )
    copies = []
    for side, (blocks, target) in enumerate(((up, up_ref), (down, down_ref))):
        for slot, block in enumerate(blocks):
            at = jnp.clip(block - z * 16, 0, 15)
            copies.append(
                pltpu.make_async_copy(
                    r_ref.at[pl.ds(at * 2, 2), pl.ds(0, KV)],
                    target.at[pl.ds(slot * 2, 2)],
                    sems.at[side * 4 + slot],
                )
            )
    for copy in copies:
        copy.start()
    for copy in copies:
        copy.wait()


def softmax(scores):
    top = jnp.max(scores, axis=0, keepdims=True)
    exponent = jnp.exp(scores - top)
    return top, jnp.sum(exponent, axis=0, keepdims=True), exponent.astype(BF)


def attend_kernel(lists, zi, r_ref, prev_ref, next_ref, out_ref, win, kg, vg, k5g, v5g, sems):
    z = zi[0]
    copies = [
        pltpu.make_async_copy(r_ref, win.at[pl.ds(0, 32)], sems.at[0]),
        pltpu.make_async_copy(prev_ref, win.at[pl.ds(32, 8), pl.ds(0, KV)], sems.at[1]),
        pltpu.make_async_copy(next_ref, win.at[pl.ds(40, 8), pl.ds(0, KV)], sems.at[2]),
    ]
    for copy in copies:
        copy.start()
    for copy in copies:
        copy.wait()
    scale = HD**-0.5
    for x in range(NX):
        near_before, near_after = jnp.int32(0), jnp.int32(0)
        biases = []
        for m in range(MAXB):
            entry = lists[(z * 4 + x) * MAXB + m]
            live = entry >= 0
            rel = entry - z * 16
            at = jnp.clip(rel, 0, 15)
            quarter = rel >> 2
            if x == 0:
                at = jnp.where(quarter == -2, 16, at)
                at = jnp.where(quarter == -1, 17 + jnp.minimum(near_before, 1), at)
                near_before = near_before + ((quarter == -1) & live).astype(jnp.int32)
            if x == 1:
                at = jnp.where(quarter == -1, 19, at)
            if x == 2:
                at = jnp.where(quarter == 4, 23, at)
            if x == 3:
                at = jnp.where(quarter == 5, 20, at)
                at = jnp.where(quarter == 4, 21 + jnp.minimum(near_after, 1), at)
                near_after = near_after + ((quarter == 4) & live).astype(jnp.int32)
            at = jnp.where(live, at, 0)
            biases.append(jnp.where(live, 0.0, -jnp.inf))
            for half in range(2):
                row = m * 2 + half
                block = win.at[at * 2 + half]
                kg[row * 64 : row * 64 + 64] = block[K0 : K0 + 64]
                vg[row * 64 : row * 64 + 64] = block[V0 : V0 + 64]
                k5g[row * 16 : row * 16 + 16] = block[K5 : K5 + 16]
                v5g[row * 16 : row * 16 + 16] = block[V5 : V5 + 16]
        cols = slice(x * 128, x * 128 + 128)
        q = win[x * NH : x * NH + NH, Q0 : Q0 + QROWS].reshape(128, HD)
        raw = dot(kg[...], q, (1, 1)) * scale
        scores = jnp.concatenate([raw[m * 128 : m * 128 + 128] + biases[m] for m in range(MAXB)], axis=0)
        top, total, weights = softmax(scores)
        out_ref[0:128, cols] = (dot(vg[...], weights, (0, 0)) / total).astype(BF)

        q5 = win[x * NH : x * NH + NH, Q5 : Q5 + QROWS].reshape(128, HD)
        raw = dot(k5g[...], q5, (1, 1)) * scale
        scores = jnp.concatenate([raw[m * 32 : m * 32 + 32] + biases[m] for m in range(MAXB)], axis=0)
        top, total, weights = softmax(scores)
        out_ref[128:256, cols] = (dot(v5g[...], weights, (0, 0)) / total).astype(BF)
        level = top + jnp.log(total)
        high = level.astype(BF)
        rest = level - high.astype(F32)
        middle = rest.astype(BF)
        low = (rest - middle.astype(F32)).astype(BF)
        zeros = jnp.zeros((13, 128), F32)
        out_ref[256:272, cols] = jnp.concatenate(
            [high.astype(F32), middle.astype(F32), low.astype(F32), zeros], axis=0
        ).astype(BF)


def project_kernel(g_ref, w_ref, out_ref, a_ref):
    levels = []
    for x in range(NX):
        parts = g_ref[x, 256:272].astype(F32)
        levels.append(parts[0:1] + parts[1:2] + parts[2:3])
    top = jnp.maximum(jnp.maximum(levels[0], levels[1]), jnp.maximum(levels[2], levels[3]))
    shares = [jnp.exp(level - top) for level in levels]
    total = shares[0] + shares[1] + shares[2] + shares[3]
    shared = jnp.zeros((128, 512), F32)
    for x in range(NX):
        a_ref[x * 128 : x * 128 + 128] = g_ref[x, 0:128]
        shared = shared + g_ref[x, 128:256].astype(F32) * (shares[x] / total)
    a_ref[512:640] = shared.astype(BF)
    a = a_ref[...]
    for group in range(NH):
        part = dot(w_ref[group * 160 : group * 160 + 160], a, (1, 0)).astype(BF)
        for x in range(NX):
            out_ref[x * NH + group] = part[:, x * 128 : x * 128 + 128]


def final_kernel(r_ref, out_ref, t_ref):
    for x in range(NX):
        total = r_ref[x * NH].astype(F32)
        for group in range(1, NH):
            total = total + r_ref[x * NH + group].astype(F32)
        t_ref[x * 80 : x * 80 + 80] = total[0:80]
        t_ref[320 + x * 80 : 320 + x * 80 + 80] = total[80:160]
    out_ref[...] = t_ref[...].T.astype(BF)


def call(kernel, out, specs, out_specs=VMEM, scratch=(), cost=None):
    return pl.pallas_call(
        kernel,
        out_shape=out,
        in_specs=specs,
        out_specs=out_specs,
        scratch_shapes=list(scratch),
        compiler_params=pltpu.CompilerParams(vmem_limit_bytes=LIMIT),
        cost_estimate=cost,
    )


def shape(*dims):
    return jax.ShapeDtypeStruct(dims, BF)


def cost(us):
    return pl.CostEstimate(flops=int(us * 1e9), bytes_accessed=1 << 20, transcendentals=0)


def per_device(query_input, key_input, value_input, query_gain, key_gain, band_lists, out_weight):
    plane = ("x", "y", "c")
    weight = lax.all_gather(out_weight.T, "z", axis=0, tiled=True)
    lists = band_lists.reshape(-1)
    zi = lax.axis_index("z").reshape(1)
    packed = call(pack_kernel, shape(32, CHUNK, HD), [VMEM] * 5)(
        query_input, key_input, value_input, query_gain.reshape(1, -1), key_gain.reshape(1, -1)
    )
    mine = lax.all_to_all(packed, plane, split_axis=0, concat_axis=0, tiled=True)
    up, down = call(
        select_kernel,
        (shape(8, KV, HD), shape(8, KV, HD)),
        [SMEM, SMEM, ANY],
        (ANY, ANY),
        [pltpu.SemaphoreType.DMA((8,))],
    )(lists, zi, mine)
    before = lax.ppermute(up, "z", [(i, i + 1) for i in range(NZ - 1)])
    after = lax.ppermute(down, "z", [(i + 1, i) for i in range(NZ - 1)])
    attended = call(
        attend_kernel,
        shape(272, 512),
        [SMEM, SMEM, ANY, ANY, ANY],
        VMEM,
        [
            pltpu.VMEM((48, CHUNK, HD), BF),
            pltpu.VMEM((1024, HD), BF),
            pltpu.VMEM((1024, HD), BF),
            pltpu.VMEM((256, HD), BF),
            pltpu.VMEM((256, HD), BF),
            pltpu.SemaphoreType.DMA((3,)),
        ],
    )(lists, zi, mine, before, after)
    gathered = lax.all_gather(attended, "x", axis=0, tiled=False)
    terms = call(project_kernel, shape(32, 160, 128), [VMEM, VMEM], VMEM, [pltpu.VMEM((640, 512), BF)])(
        gathered, weight
    )
    summands = lax.all_to_all(terms, plane, split_axis=0, concat_axis=0, tiled=True)
    return call(final_kernel, shape(128, 640), [VMEM], VMEM, [pltpu.VMEM((640, 128), F32)])(summands)


def solution(mesh):
    split = Mesh(mesh.devices.reshape(NZ, NX, 4, 2), ("z", "x", "y", "c"))
    rows = P(("z", "x", "y", "c"), None)
    return jax.shard_map(
        per_device,
        mesh=split,
        in_specs=(rows, rows, rows, P(), P(), P(), P(("y", "c"), ("z", "x"))),
        out_specs=P(("z", "x"), ("y", "c")),
        check_vma=False,
    )
```

```python
import jax
import jax.numpy as jnp
from jax import lax
from jax.experimental import pallas as pl
from jax.experimental.pallas import tpu as pltpu
from jax.sharding import Mesh, PartitionSpec as P

HD = 128
D = 5120
HALF = 64
QROWS = 16
NX = 4
NH = 8
NZ = 16
MAXB = 8
GROUP = 5
K0, V0, K5, V5, Q0, Q5, CHUNK = 0, 64, 128, 144, 160, 176, 192
KV = 160
BF = jnp.bfloat16
F32 = jnp.float32
VMEM = pl.BlockSpec(memory_space=pltpu.VMEM)
SMEM = pl.BlockSpec(memory_space=pltpu.SMEM)
ANY = pl.BlockSpec(memory_space=pl.ANY)
LIMIT = 40 * 1024 * 1024
ALL = 60 * 1024 * 1024
FAR_STEPS = (4, 0, -4, 8)
NEAR_STEPS = (0, 1, -1, 2, -2)
NEAR_COUNT = (4, 4, 4, 2, 2)
PLACES = [(i, FAR_STEPS[(1 if step == -2 else 0) + j]) for i, step in enumerate(NEAR_STEPS) for j in range(NEAR_COUNT[i])]


def dot(a, b, contract):
    return lax.dot_general(a, b, ((contract[:1], contract[1:]), ((), ())), preferred_element_type=F32)


def pack_kernel(q_hbm, k_hbm, v_hbm, qg_hbm, kg_hbm, out_ref, q_ref, k_ref, v_ref, qg_ref, kg_ref, sems):
    pairs = ((k_hbm, k_ref), (kg_hbm, kg_ref), (q_hbm, q_ref), (qg_hbm, qg_ref), (v_hbm, v_ref))
    copies = [pltpu.make_async_copy(*pair, sems.at[i]) for i, pair in enumerate(pairs)]
    for copy in copies:
        copy.start()
    for copy in copies:
        copy.wait()

    def inverse(ref):
        wide = ref[...].astype(F32)
        return lax.rsqrt(jnp.mean(wide * wide, axis=-1, keepdims=True) + 1e-06)

    q_inv, k_inv = inverse(q_ref), inverse(k_ref)
    for group in range(NH):
        for at in range(GROUP):
            cols = slice((group * GROUP + at) * HD, (group * GROUP + at + 1) * HD)
            q = (q_ref[:, cols].astype(F32) * q_inv * qg_ref[:, cols]).astype(BF)
            k = (k_ref[:, cols].astype(F32) * k_inv * kg_ref[:, cols]).astype(BF)
            v = v_ref[:, cols]
            if at < NX:
                chunk = at * NH + group
                out_ref[chunk, K0 : K0 + HALF] = k
                out_ref[chunk, V0 : V0 + HALF] = v
                out_ref[chunk, Q0 : Q0 + QROWS] = q
            else:
                for x in range(NX):
                    chunk = x * NH + group
                    rows = slice(x * 16, x * 16 + 16)
                    out_ref[chunk, K5 : K5 + 16] = k[rows]
                    out_ref[chunk, V5 : V5 + 16] = v[rows]
                    out_ref[chunk, Q5 : Q5 + QROWS] = q


def listed_of(lists, block, seq, count):
    found = [jnp.int32(-1)] * count
    for m in range(MAXB):
        entry = lists[block * MAXB + m]
        hit = (entry >= 0) & ((entry >> 2) == seq)
        for i in reversed(range(count)):
            free = found[i] < 0
            if i:
                free = free & (found[i - 1] >= 0)
            found[i] = jnp.where(hit & free, entry, found[i])
    return found


def select_kernel(lists, zi, r_ref, first_columns, up_ref, down_ref, sems):
    del first_columns
    z = zi[0]
    above = jnp.minimum(z + 1, NZ - 1) * 4
    below = jnp.maximum(z - 1, 0) * 4
    first = z * 4
    up = (
        listed_of(lists, above, first + 2, 1)
        + listed_of(lists, above, first + 3, 2)
        + listed_of(lists, above + 1, first + 3, 1)
    )
    down = (
        listed_of(lists, below + 3, first + 1, 1)
        + listed_of(lists, below + 3, first, 2)
        + listed_of(lists, below + 2, first, 1)
    )
    copies = []
    for side, (blocks, target) in enumerate(((up, up_ref), (down, down_ref))):
        for slot, block in enumerate(blocks):
            at = jnp.clip(block - z * 16, 0, 15)
            copies.append(
                pltpu.make_async_copy(
                    r_ref.at[pl.ds(at * 2, 2), pl.ds(0, KV)],
                    target.at[pl.ds(slot * 2, 2)],
                    sems.at[side * 4 + slot],
                )
            )
    for copy in copies:
        copy.start()
    for copy in copies:
        copy.wait()


def softmax(scores):
    top = jnp.max(scores, axis=0, keepdims=True)
    exponent = jnp.exp(scores - top)
    return top, jnp.sum(exponent, axis=0, keepdims=True), exponent.astype(BF)


def attend_kernel(lists, zi, r_ref, prev_ref, next_ref, out_ref, win, kg, vg, k5g, v5g, sems):
    z = zi[0]
    copies = [
        pltpu.make_async_copy(r_ref, win.at[pl.ds(0, 32)], sems.at[0]),
        pltpu.make_async_copy(prev_ref, win.at[pl.ds(32, 8), pl.ds(0, KV)], sems.at[1]),
        pltpu.make_async_copy(next_ref, win.at[pl.ds(40, 8), pl.ds(0, KV)], sems.at[2]),
    ]
    for copy in copies:
        copy.start()
    for copy in copies:
        copy.wait()
    scale = HD**-0.5
    for x in range(NX):
        near_before, near_after = jnp.int32(0), jnp.int32(0)
        biases = []
        for m in range(MAXB):
            entry = lists[(z * 4 + x) * MAXB + m]
            live = entry >= 0
            rel = entry - z * 16
            at = jnp.clip(rel, 0, 15)
            quarter = rel >> 2
            if x == 0:
                at = jnp.where(quarter == -2, 16, at)
                at = jnp.where(quarter == -1, 17 + jnp.minimum(near_before, 1), at)
                near_before = near_before + ((quarter == -1) & live).astype(jnp.int32)
            if x == 1:
                at = jnp.where(quarter == -1, 19, at)
            if x == 2:
                at = jnp.where(quarter == 4, 23, at)
            if x == 3:
                at = jnp.where(quarter == 5, 20, at)
                at = jnp.where(quarter == 4, 21 + jnp.minimum(near_after, 1), at)
                near_after = near_after + ((quarter == 4) & live).astype(jnp.int32)
            at = jnp.where(live, at, 0)
            biases.append(jnp.where(live, 0.0, -jnp.inf))
            for half in range(2):
                row = m * 2 + half
                block = win.at[at * 2 + half]
                kg[row * 64 : row * 64 + 64] = block[K0 : K0 + 64]
                vg[row * 64 : row * 64 + 64] = block[V0 : V0 + 64]
                k5g[row * 16 : row * 16 + 16] = block[K5 : K5 + 16]
                v5g[row * 16 : row * 16 + 16] = block[V5 : V5 + 16]
        cols = slice(x * 128, x * 128 + 128)
        q = win[x * NH : x * NH + NH, Q0 : Q0 + QROWS].reshape(128, HD)
        raw = dot(kg[...], q, (1, 1)) * scale
        scores = jnp.concatenate([raw[m * 128 : m * 128 + 128] + biases[m] for m in range(MAXB)], axis=0)
        top, total, weights = softmax(scores)
        own = (dot(vg[...], weights, (0, 0)) / total).astype(BF)

        q5 = win[x * NH : x * NH + NH, Q5 : Q5 + QROWS].reshape(128, HD)
        raw = dot(k5g[...], q5, (1, 1)) * scale
        scores = jnp.concatenate([raw[m * 32 : m * 32 + 32] + biases[m] for m in range(MAXB)], axis=0)
        top, total, weights = softmax(scores)
        shared = (dot(v5g[...], weights, (0, 0)) / total).astype(BF)
        level = top + jnp.log(total)
        high = level.astype(BF)
        rest = level - high.astype(F32)
        middle = rest.astype(BF)
        low = (rest - middle.astype(F32)).astype(BF)
        zeros = jnp.zeros((13, 128), F32)
        pieces = jnp.concatenate([high.astype(F32), middle.astype(F32), low.astype(F32), zeros], axis=0).astype(BF)
        for target in range(NX):
            out_ref[target, 0:128, cols] = own
            out_ref[target, 128:256, cols] = shared
            out_ref[target, 256:272, cols] = pieces


def project_kernel(zi, g_hbm, *rest):
    weights, (out_ref, g_ref, w_ref, a_ref, sems) = rest[:5], rest[5:]
    copies = [pltpu.make_async_copy(g_hbm, g_ref, sems.at[5])]
    for i, w_hbm in enumerate(weights):
        at = sum(NEAR_COUNT[:i])
        copies.append(pltpu.make_async_copy(w_hbm, w_ref.at[pl.ds(at, NEAR_COUNT[i])], sems.at[i]))
    for copy in copies:
        copy.start()
    for copy in copies:
        copy.wait()
    levels = []
    for x in range(NX):
        parts = g_ref[x, 256:272].astype(F32)
        levels.append(parts[0:1] + parts[1:2] + parts[2:3])
    top = jnp.maximum(jnp.maximum(levels[0], levels[1]), jnp.maximum(levels[2], levels[3]))
    shares = [jnp.exp(level - top) for level in levels]
    total = shares[0] + shares[1] + shares[2] + shares[3]
    shared = jnp.zeros((128, 512), F32)
    for x in range(NX):
        a_ref[x * 128 : x * 128 + 128] = g_ref[x, 0:128]
        shared = shared + g_ref[x, 128:256].astype(F32) * (shares[x] / total)
    a_ref[512:640] = shared.astype(BF)
    a = a_ref[...]
    for place, (near, stride) in enumerate(PLACES):
        part = dot(w_ref[place], a, (1, 0)).astype(BF)
        source = (zi[0] + NEAR_STEPS[near] + stride) & (NZ - 1)
        rows = pl.ds(pl.multiple_of((source & 1) * 80, 80), 80)
        for x in range(NX):
            out_ref[x * NH + (source >> 1), rows] = part[:, x * 128 : x * 128 + 128]


def final_kernel(r_ref, out_ref, t_ref):
    for x in range(NX):
        total = r_ref[x * NH].astype(F32)
        for group in range(1, NH):
            total = total + r_ref[x * NH + group].astype(F32)
        t_ref[x * 80 : x * 80 + 80] = total[0:80]
        t_ref[320 + x * 80 : 320 + x * 80 + 80] = total[80:160]
    out_ref[...] = t_ref[...].T.astype(BF)


def call(kernel, out, specs, out_specs=VMEM, scratch=(), limit=LIMIT):
    return pl.pallas_call(
        kernel,
        out_shape=out,
        in_specs=specs,
        out_specs=out_specs,
        scratch_shapes=list(scratch),
        compiler_params=pltpu.CompilerParams(vmem_limit_bytes=limit),
    )


def shape(*dims):
    return jax.ShapeDtypeStruct(dims, BF)


def from_plane(value, step):
    return lax.ppermute(value, "z", [((i + step) % NZ, i) for i in range(NZ)])


def per_device(query_input, key_input, value_input, query_gain, key_gain, band_lists, out_weight):
    plane = ("x", "y", "c")
    lists = band_lists.reshape(-1)
    zi = lax.axis_index("z").reshape(1)
    packed = call(
        pack_kernel,
        shape(32, CHUNK, HD),
        [ANY] * 5,
        VMEM,
        [
            pltpu.VMEM((QROWS, D), BF),
            pltpu.VMEM((HALF, D), BF),
            pltpu.VMEM((HALF, D), BF),
            pltpu.VMEM((1, D), F32),
            pltpu.VMEM((1, D), F32),
            pltpu.SemaphoreType.DMA((5,)),
        ],
        ALL,
    )(query_input, key_input, value_input, query_gain.reshape(1, -1), key_gain.reshape(1, -1))
    packed, columns = lax.optimization_barrier((packed, out_weight.T))
    far = jnp.stack([from_plane(columns, step) if step else columns for step in FAR_STEPS])
    near = [far, from_plane(far, 1), from_plane(far, -1), from_plane(far[:2], 2), from_plane(far[1:3], -2)]
    mine = lax.all_to_all(packed, plane, split_axis=0, concat_axis=0, tiled=True)
    up, down = call(
        select_kernel,
        (shape(8, KV, HD), shape(8, KV, HD)),
        [SMEM, SMEM, ANY, ANY],
        (ANY, ANY),
        [pltpu.SemaphoreType.DMA((8,))],
    )(lists, zi, mine, far)
    before = lax.ppermute(up, "z", [(i, i + 1) for i in range(NZ - 1)])
    after = lax.ppermute(down, "z", [(i + 1, i) for i in range(NZ - 1)])
    attended = call(
        attend_kernel,
        shape(NX, 272, 512),
        [SMEM, SMEM, ANY, ANY, ANY],
        VMEM,
        [
            pltpu.VMEM((48, CHUNK, HD), BF),
            pltpu.VMEM((1024, HD), BF),
            pltpu.VMEM((1024, HD), BF),
            pltpu.VMEM((256, HD), BF),
            pltpu.VMEM((256, HD), BF),
            pltpu.SemaphoreType.DMA((3,)),
        ],
    )(lists, zi, mine, before, after)
    gathered = lax.all_to_all(attended, "x", split_axis=0, concat_axis=0, tiled=True)
    terms = call(
        project_kernel,
        shape(32, 160, 128),
        [SMEM] + [ANY] * 6,
        VMEM,
        [
            pltpu.VMEM((NX, 272, 512), BF),
            pltpu.VMEM((NZ, 80, 640), BF),
            pltpu.VMEM((640, 512), BF),
            pltpu.SemaphoreType.DMA((6,)),
        ],
    )(zi, gathered, *near)
    summands = lax.all_to_all(terms, plane, split_axis=0, concat_axis=0, tiled=True)
    return call(final_kernel, shape(128, 640), [VMEM], VMEM, [pltpu.VMEM((640, 128), F32)])(summands)


def solution(mesh):
    split = Mesh(mesh.devices.reshape(NZ, NX, 4, 2), ("z", "x", "y", "c"))
    rows = P(("z", "x", "y", "c"), None)
    return jax.shard_map(
        per_device,
        mesh=split,
        in_specs=(rows, rows, rows, P(), P(), P(), P(("y", "c"), ("z", "x"))),
        out_specs=P(("z", "x"), ("y", "c")),
        check_vma=False,
    )
```

```python
import jax
import jax.numpy as jnp
from jax import lax
from jax.experimental import pallas as pl
from jax.experimental.pallas import tpu as pltpu
from jax.sharding import Mesh, PartitionSpec as P

HD = 128
D = 5120
HALF = 64
QROWS = 16
NX = 4
NH = 8
NZ = 16
MAXB = 8
GROUP = 5
K0, V0, K5, V5, Q0, Q5, CHUNK = 0, 64, 128, 144, 160, 176, 192
KV = 160
BF = jnp.bfloat16
F32 = jnp.float32
VMEM = pl.BlockSpec(memory_space=pltpu.VMEM)
SMEM = pl.BlockSpec(memory_space=pltpu.SMEM)
ANY = pl.BlockSpec(memory_space=pl.ANY)
LIMIT = 40 * 1024 * 1024
ALL = 60 * 1024 * 1024
HELD = (0, 5, -6)
LAST = -3
BLOCK = 400
SK, SV, SK5, SV5, SW = 0, 512, 1024, 1152, 1280
SENT = SW + 3 * BLOCK


def dot(a, b, contract):
    return lax.dot_general(a, b, ((contract[:1], contract[1:]), ((), ())), preferred_element_type=F32)


def pack_kernel(q_hbm, k_hbm, v_hbm, qg_hbm, kg_hbm, out_ref, q_ref, k_ref, v_ref, qg_ref, kg_ref, sems):
    pairs = ((k_hbm, k_ref), (kg_hbm, kg_ref), (q_hbm, q_ref), (qg_hbm, qg_ref), (v_hbm, v_ref))
    copies = [pltpu.make_async_copy(*pair, sems.at[i]) for i, pair in enumerate(pairs)]
    for copy in copies:
        copy.start()
    for copy in copies[:4]:
        copy.wait()

    def inverse(ref):
        wide = ref[...].astype(F32)
        return lax.rsqrt(jnp.mean(wide * wide, axis=-1, keepdims=True) + 1e-06)

    k_inv, q_inv = inverse(k_ref), inverse(q_ref)

    def heads():
        for group in range(NH):
            for at in range(GROUP):
                yield group, at, slice((group * GROUP + at) * HD, (group * GROUP + at + 1) * HD)

    for group, at, cols in heads():
        k = (k_ref[:, cols].astype(F32) * k_inv * kg_ref[:, cols]).astype(BF)
        q = (q_ref[:, cols].astype(F32) * q_inv * qg_ref[:, cols]).astype(BF)
        if at < NX:
            out_ref[at * NH + group, K0 : K0 + HALF] = k
            out_ref[at * NH + group, Q0 : Q0 + QROWS] = q
        else:
            for x in range(NX):
                out_ref[x * NH + group, K5 : K5 + 16] = k[x * 16 : x * 16 + 16]
                out_ref[x * NH + group, Q5 : Q5 + QROWS] = q
    copies[4].wait()
    for group, at, cols in heads():
        if at < NX:
            out_ref[at * NH + group, V0 : V0 + HALF] = v_ref[:, cols]
        else:
            for x in range(NX):
                out_ref[x * NH + group, V5 : V5 + 16] = v_ref[x * 16 : x * 16 + 16, cols]


def listed_of(lists, block, seq, count):
    found = [jnp.int32(-1)] * count
    for m in range(MAXB):
        entry = lists[block * MAXB + m]
        hit = (entry >= 0) & ((entry >> 2) == seq)
        for i in reversed(range(count)):
            free = found[i] < 0
            if i:
                free = free & (found[i - 1] >= 0)
            found[i] = jnp.where(hit & free, entry, found[i])
    return found


def listed_above(lists, z):
    block = jnp.minimum(z + 1, NZ - 1) * 4
    seq = z * 4
    return (
        listed_of(lists, block, seq + 2, 1) + listed_of(lists, block, seq + 3, 2) + listed_of(lists, block + 1, seq + 3, 1)
    )


def listed_below(lists, z):
    block = jnp.maximum(z - 1, 0) * 4
    seq = z * 4
    return (
        listed_of(lists, block + 3, seq + 1, 1) + listed_of(lists, block + 3, seq, 2) + listed_of(lists, block + 2, seq, 1)
    )


def select_kernel(lists, zi, r_ref, *rest):
    held, (up_ref, down_ref) = rest[:3], rest[3:]
    z = zi[0]
    for blocks, target in ((listed_above(lists, z), up_ref), (listed_below(lists, z), down_ref)):
        for slot, block in enumerate(blocks):
            at = jnp.clip(block - z * 16, 0, 15)
            for half in range(2):
                source, part = r_ref.at[at * 2 + half], slot * 2 + half
                target[SK + part * 64 : SK + part * 64 + 64] = source[K0 : K0 + 64]
                target[SV + part * 64 : SV + part * 64 + 64] = source[V0 : V0 + 64]
                target[SK5 + part * 16 : SK5 + part * 16 + 16] = source[K5 : K5 + 16]
                target[SV5 + part * 16 : SV5 + part * 16 + 16] = source[V5 : V5 + 16]
        for i, ref in enumerate(held):
            target[SW + i * BLOCK : SW + i * BLOCK + BLOCK] = ref[...]


def queries(r_ref, x, first):
    return r_ref[x * NH : x * NH + NH, first : first + QROWS].reshape(128, HD)


def scored(keys, q, biases):
    raw = dot(keys, q, (1, 1)) * HD**-0.5
    rows = keys.shape[0] // len(biases)
    return jnp.concatenate([raw[i * rows : i * rows + rows] + bias for i, bias in enumerate(biases)], axis=0)


def attend_own_kernel(lists, zi, r_ref, sum_ref, stat_ref, kg, vg, k5g, v5g):
    z = zi[0]
    for x in range(NX):
        biases = []
        for m in range(MAXB):
            entry = lists[(z * 4 + x) * MAXB + m]
            here = (entry >> 4) == z
            at = jnp.where(here, entry - z * 16, 0)
            biases.append(jnp.where(here, 0.0, -jnp.inf))
            for half in range(2):
                row = m * 2 + half
                block = r_ref.at[at * 2 + half]
                kg[row * 64 : row * 64 + 64] = block[K0 : K0 + 64]
                vg[row * 64 : row * 64 + 64] = block[V0 : V0 + 64]
                k5g[row * 16 : row * 16 + 16] = block[K5 : K5 + 16]
                v5g[row * 16 : row * 16 + 16] = block[V5 : V5 + 16]
        cols = slice(x * 128, x * 128 + 128)
        for i, (keys, values, first) in enumerate(((kg, vg, Q0), (k5g, v5g, Q5))):
            scores = scored(keys[...], queries(r_ref, x, first), biases)
            top = jnp.max(scores, axis=0, keepdims=True)
            exponent = jnp.exp(scores - top)
            stat_ref[i * 2 : i * 2 + 1, cols] = top
            stat_ref[i * 2 + 1 : i * 2 + 2, cols] = jnp.sum(exponent, axis=0, keepdims=True)
            sum_ref[i * 128 : i * 128 + 128, cols] = dot(values[...], exponent.astype(BF), (0, 0))


def attend_rest_kernel(lists, zi, r_ref, prev_ref, next_ref, sum_ref, stat_ref, last, out_ref, above_ref, below_ref):
    del last
    z = zi[0]
    below_ref[...] = prev_ref[SW:]
    above_ref[...] = next_ref[SW:]
    near = listed_above(lists, z - 1), listed_below(lists, z + 1)
    for x in range(NX):
        ref, side = ((prev_ref, 0), (next_ref, 1))[x // 2]
        first, count = (0, 3) if x in (0, 3) else (3, 1)
        found = near[side][first : first + count]
        inside = (z > 0) if side == 0 else (z < NZ - 1)
        biases = [jnp.where((block >= 0) & inside, 0.0, -jnp.inf) for block in found]
        cols = slice(x * 128, x * 128 + 128)
        for i, (key_row, value_row, size, query_row) in enumerate(((SK, SV, 128, Q0), (SK5, SV5, 32, Q5))):
            keys = ref[key_row + first * size : key_row + (first + count) * size]
            values = ref[value_row + first * size : value_row + (first + count) * size]
            scores = scored(keys, queries(r_ref, x, query_row), biases)
            old = stat_ref[i * 2 : i * 2 + 1, cols]
            top = jnp.maximum(old, jnp.max(scores, axis=0, keepdims=True))
            exponent = jnp.exp(scores - top)
            share = jnp.exp(old - top)
            total = stat_ref[i * 2 + 1 : i * 2 + 2, cols] * share + jnp.sum(exponent, axis=0, keepdims=True)
            added = sum_ref[i * 128 : i * 128 + 128, cols] * share + dot(values, exponent.astype(BF), (0, 0))
            result = (added / total).astype(BF)
            for target in range(NX):
                out_ref[target, i * 128 : i * 128 + 128, cols] = result
        level = top + jnp.log(total)
        high = level.astype(BF)
        left = level - high.astype(F32)
        middle = left.astype(BF)
        low = (left - middle.astype(F32)).astype(BF)
        zeros = jnp.zeros((13, 128), F32)
        pieces = jnp.concatenate([high.astype(F32), middle.astype(F32), low.astype(F32), zeros], axis=0).astype(BF)
        for target in range(NX):
            out_ref[target, 256:272, cols] = pieces


def project_kernel(ci, zi, g_ref, own, up5, down6, last, before, after, before2, after2, keep_ref, give_ref, a_ref, w_ref):
    blocks = [(last, 0, LAST)] + [(ref, 0, step) for ref, step in zip((own, up5, down6), HELD)]
    for ref, step in ((before, -1), (after, 1), (before2, -2), (after2, 2)):
        blocks += [(ref, i * BLOCK, step + offset) for i, offset in enumerate(HELD)]
    for ref, first, step in blocks:
        rows = pl.ds(pl.multiple_of(((zi[0] + step) & (NZ - 1)) * 80, 80), 80)
        for head in range(GROUP):
            w_ref[rows, head * HD : head * HD + HD] = ref[first + head * 80 : first + head * 80 + 80]
    levels = []
    for x in range(NX):
        parts = g_ref[x, 256:272].astype(F32)
        levels.append(parts[0:1] + parts[1:2] + parts[2:3])
    top = jnp.maximum(jnp.maximum(levels[0], levels[1]), jnp.maximum(levels[2], levels[3]))
    shares = [jnp.exp(level - top) for level in levels]
    total = shares[0] + shares[1] + shares[2] + shares[3]
    shared = jnp.zeros((128, 512), F32)
    for x in range(NX):
        a_ref[x * 128 : x * 128 + 128] = g_ref[x, 0:128]
        shared = shared + g_ref[x, 128:256].astype(F32) * (shares[x] / total)
    a_ref[512:640] = shared.astype(BF)
    a = a_ref[...]
    for other, target in ((1, give_ref), (0, keep_ref)):
        parity = ci[0] ^ other
        for y in range(4):
            rows = pl.ds(pl.multiple_of((2 * y + parity) * 160, 160), 160)
            part = dot(w_ref[rows], a, (1, 0)).astype(BF)
            for x in range(NX):
                target[x * 4 + y] = part[:, x * 128 : x * 128 + 128]


def final_kernel(r_ref, out_ref, t_ref):
    for x in range(NX):
        total = r_ref[x * 4].astype(F32)
        for y in range(1, 4):
            total = total + r_ref[x * 4 + y].astype(F32)
        t_ref[x * 80 : x * 80 + 80] = total[0:80]
        t_ref[320 + x * 80 : 320 + x * 80 + 80] = total[80:160]
    out_ref[...] = t_ref[...].T.astype(BF)


def call(kernel, out, specs, out_specs=VMEM, scratch=(), limit=LIMIT):
    return pl.pallas_call(
        kernel,
        out_shape=out,
        in_specs=specs,
        out_specs=out_specs,
        scratch_shapes=list(scratch),
        compiler_params=pltpu.CompilerParams(vmem_limit_bytes=limit),
    )


def shape(*dims):
    return jax.ShapeDtypeStruct(dims, BF)


def from_plane(value, step):
    return lax.ppermute(value, "z", [((i + step) % NZ, i) for i in range(NZ)])


def per_device(query_input, key_input, value_input, query_gain, key_gain, band_lists, out_weight):
    plane = ("x", "y", "c")
    lists = band_lists.reshape(-1)
    zi = lax.axis_index("z").reshape(1)
    packed = call(
        pack_kernel,
        shape(32, CHUNK, HD),
        [ANY] * 5,
        VMEM,
        [
            pltpu.VMEM((QROWS, D), BF),
            pltpu.VMEM((HALF, D), BF),
            pltpu.VMEM((HALF, D), BF),
            pltpu.VMEM((1, D), F32),
            pltpu.VMEM((1, D), F32),
            pltpu.SemaphoreType.DMA((5,)),
        ],
        ALL,
    )(query_input, key_input, value_input, query_gain.reshape(1, -1), key_gain.reshape(1, -1))
    packed, columns = lax.optimization_barrier((packed, out_weight))
    columns = columns.reshape(GROUP, HD, 80).transpose(0, 2, 1).reshape(BLOCK, HD)
    held = [columns] + [from_plane(columns, step) for step in HELD[1:]]
    mine = lax.all_to_all(packed, plane, split_axis=0, concat_axis=0, tiled=True)
    up, down = call(
        select_kernel, (shape(SENT, HD), shape(SENT, HD)), [SMEM, SMEM] + [VMEM] * 4, (VMEM, VMEM)
    )(lists, zi, mine, *held)
    before, after = from_plane(up, -1), from_plane(down, 1)
    last = from_plane(columns, LAST)
    sums, stats = call(
        attend_own_kernel,
        (jax.ShapeDtypeStruct((256, 512), F32), jax.ShapeDtypeStruct((8, 512), F32)),
        [SMEM, SMEM, VMEM],
        (VMEM, VMEM),
        [pltpu.VMEM((1024, HD), BF), pltpu.VMEM((1024, HD), BF), pltpu.VMEM((256, HD), BF), pltpu.VMEM((256, HD), BF)],
    )(lists, zi, mine)
    attended, above_w, below_w = call(
        attend_rest_kernel,
        (shape(NX, 272, 512), shape(3 * BLOCK, HD), shape(3 * BLOCK, HD)),
        [SMEM, SMEM] + [VMEM] * 5 + [ANY],
        (VMEM, VMEM, VMEM),
    )(lists, zi, mine, before, after, sums, stats, last)
    below2, above2 = from_plane(below_w, -1), from_plane(above_w, 1)
    gathered = lax.all_to_all(attended, "x", split_axis=0, concat_axis=0, tiled=True)
    ci = lax.axis_index("c").reshape(1)
    keep, give = call(
        project_kernel,
        (shape(16, 160, 128), shape(16, 160, 128)),
        [SMEM, SMEM] + [VMEM] * 9,
        (VMEM, VMEM),
        [pltpu.VMEM((640, 512), BF), pltpu.VMEM((NZ * 80, 640), BF)],
    )(ci, zi, gathered, *held, last, below_w, above_w, below2, above2)
    other = lax.ppermute(give, "c", [(0, 1), (1, 0)])
    terms = (keep.astype(F32) + other.astype(F32)).astype(BF)
    summands = lax.all_to_all(terms, ("x", "y"), split_axis=0, concat_axis=0, tiled=True)
    return call(final_kernel, shape(128, 640), [VMEM], VMEM, [pltpu.VMEM((640, 128), F32)])(summands)


def solution(mesh):
    split = Mesh(mesh.devices.reshape(NZ, NX, 4, 2), ("z", "x", "y", "c"))
    rows = P(("z", "x", "y", "c"), None)
    return jax.shard_map(
        per_device,
        mesh=split,
        in_specs=(rows, rows, rows, P(), P(), P(), P(("y", "c"), ("z", "x"))),
        out_specs=P(("z", "x"), ("y", "c")),
        check_vma=False,
    )
```

```python
import jax
import jax.numpy as jnp
from jax import lax
from jax.experimental import pallas as pl
from jax.experimental.pallas import tpu as pltpu
from jax.sharding import Mesh, PartitionSpec as P

HD = 128
D = 5120
HALF = 64
QROWS = 16
NX = 4
NH = 8
NZ = 16
MAXB = 8
GROUP = 5
K0, V0, K5, V5, Q0, Q5, CHUNK = 0, 64, 128, 144, 160, 176, 192
KV = 160
BF = jnp.bfloat16
F32 = jnp.float32
VMEM = pl.BlockSpec(memory_space=pltpu.VMEM)
SMEM = pl.BlockSpec(memory_space=pltpu.SMEM)
ANY = pl.BlockSpec(memory_space=pl.ANY)
LIMIT = 40 * 1024 * 1024
ALL = 60 * 1024 * 1024
HELD = (0, 5, -6)
LAST = -3
BLOCK = 400
SK, SV, SK5, SV5, SENT = 0, 512, 1024, 1152, 1280


def dot(a, b, contract):
    return lax.dot_general(a, b, ((contract[:1], contract[1:]), ((), ())), preferred_element_type=F32)


def pack_kernel(q_hbm, k_hbm, v_hbm, qg_hbm, kg_hbm, out_ref, q_ref, k_ref, v_ref, qg_ref, kg_ref, sems):
    pairs = ((k_hbm, k_ref), (kg_hbm, kg_ref), (q_hbm, q_ref), (qg_hbm, qg_ref), (v_hbm, v_ref))
    copies = [pltpu.make_async_copy(*pair, sems.at[i]) for i, pair in enumerate(pairs)]
    for copy in copies:
        copy.start()
    for copy in copies[:4]:
        copy.wait()

    def inverse(ref):
        wide = ref[...].astype(F32)
        return lax.rsqrt(jnp.mean(wide * wide, axis=-1, keepdims=True) + 1e-06)

    k_inv, q_inv = inverse(k_ref), inverse(q_ref)

    def heads():
        for group in range(NH):
            for at in range(GROUP):
                yield group, at, slice((group * GROUP + at) * HD, (group * GROUP + at + 1) * HD)

    for group, at, cols in heads():
        k = (k_ref[:, cols].astype(F32) * k_inv * kg_ref[:, cols]).astype(BF)
        q = (q_ref[:, cols].astype(F32) * q_inv * qg_ref[:, cols]).astype(BF)
        if at < NX:
            out_ref[at * NH + group, K0 : K0 + HALF] = k
            out_ref[at * NH + group, Q0 : Q0 + QROWS] = q
        else:
            for x in range(NX):
                out_ref[x * NH + group, K5 : K5 + 16] = k[x * 16 : x * 16 + 16]
                out_ref[x * NH + group, Q5 : Q5 + QROWS] = q
    copies[4].wait()
    for group, at, cols in heads():
        if at < NX:
            out_ref[at * NH + group, V0 : V0 + HALF] = v_ref[:, cols]
        else:
            for x in range(NX):
                out_ref[x * NH + group, V5 : V5 + 16] = v_ref[x * 16 : x * 16 + 16, cols]


def listed_of(lists, block, seq, count):
    found = [jnp.int32(-1)] * count
    for m in range(MAXB):
        entry = lists[block * MAXB + m]
        hit = (entry >= 0) & ((entry >> 2) == seq)
        for i in reversed(range(count)):
            free = found[i] < 0
            if i:
                free = free & (found[i - 1] >= 0)
            found[i] = jnp.where(hit & free, entry, found[i])
    return found


def listed_above(lists, z):
    block = jnp.minimum(z + 1, NZ - 1) * 4
    seq = z * 4
    return (
        listed_of(lists, block, seq + 2, 1) + listed_of(lists, block, seq + 3, 2) + listed_of(lists, block + 1, seq + 3, 1)
    )


def listed_below(lists, z):
    block = jnp.maximum(z - 1, 0) * 4
    seq = z * 4
    return (
        listed_of(lists, block + 3, seq + 1, 1) + listed_of(lists, block + 3, seq, 2) + listed_of(lists, block + 2, seq, 1)
    )


def select_kernel(lists, zi, r_ref, *rest):
    held, (up_ref, down_ref, joined_ref) = rest[:3], rest[4:]
    for i, ref in enumerate(held):
        joined_ref[i * BLOCK : i * BLOCK + BLOCK] = ref[...]
    z = zi[0]
    for blocks, target in ((listed_above(lists, z), up_ref), (listed_below(lists, z), down_ref)):
        for slot, block in enumerate(blocks):
            at = jnp.clip(block - z * 16, 0, 15)
            for half in range(2):
                source, part = r_ref.at[at * 2 + half], slot * 2 + half
                target[SK + part * 64 : SK + part * 64 + 64] = source[K0 : K0 + 64]
                target[SV + part * 64 : SV + part * 64 + 64] = source[V0 : V0 + 64]
                target[SK5 + part * 16 : SK5 + part * 16 + 16] = source[K5 : K5 + 16]
                target[SV5 + part * 16 : SV5 + part * 16 + 16] = source[V5 : V5 + 16]


def queries(r_ref, x, first):
    return r_ref[x * NH : x * NH + NH, first : first + QROWS].reshape(128, HD)


def scored(keys, q, biases):
    raw = dot(keys, q, (1, 1)) * HD**-0.5
    rows = keys.shape[0] // len(biases)
    return jnp.concatenate([raw[i * rows : i * rows + rows] + bias for i, bias in enumerate(biases)], axis=0)


def attend_own_kernel(lists, zi, r_ref, sum_ref, stat_ref, kg, vg, k5g, v5g):
    z = zi[0]
    for x in range(NX):
        biases = []
        for m in range(MAXB):
            entry = lists[(z * 4 + x) * MAXB + m]
            here = (entry >> 4) == z
            at = jnp.where(here, entry - z * 16, 0)
            biases.append(jnp.where(here, 0.0, -jnp.inf))
            for half in range(2):
                row = m * 2 + half
                block = r_ref.at[at * 2 + half]
                kg[row * 64 : row * 64 + 64] = block[K0 : K0 + 64]
                vg[row * 64 : row * 64 + 64] = block[V0 : V0 + 64]
                k5g[row * 16 : row * 16 + 16] = block[K5 : K5 + 16]
                v5g[row * 16 : row * 16 + 16] = block[V5 : V5 + 16]
        cols = slice(x * 128, x * 128 + 128)
        for i, (keys, values, first) in enumerate(((kg, vg, Q0), (k5g, v5g, Q5))):
            scores = scored(keys[...], queries(r_ref, x, first), biases)
            top = jnp.max(scores, axis=0, keepdims=True)
            exponent = jnp.exp(scores - top)
            stat_ref[i * 2 : i * 2 + 1, cols] = top
            stat_ref[i * 2 + 1 : i * 2 + 2, cols] = jnp.sum(exponent, axis=0, keepdims=True)
            sum_ref[i * 128 : i * 128 + 128, cols] = dot(values[...], exponent.astype(BF), (0, 0))


def attend_rest_kernel(lists, zi, r_ref, prev_ref, next_ref, sum_ref, stat_ref, out_ref):
    z = zi[0]
    near = listed_above(lists, z - 1), listed_below(lists, z + 1)
    parts = []
    for x in range(NX):
        ref, side = ((prev_ref, 0), (next_ref, 1))[x // 2]
        first, count = (0, 3) if x in (0, 3) else (3, 1)
        found = near[side][first : first + count]
        inside = (z > 0) if side == 0 else (z < NZ - 1)
        biases = [jnp.where((block >= 0) & inside, 0.0, -jnp.inf) for block in found]
        for i, (key_row, value_row, size, query_row) in enumerate(((SK, SV, 128, Q0), (SK5, SV5, 32, Q5))):
            keys = ref[key_row + first * size : key_row + (first + count) * size]
            values = ref[value_row + first * size : value_row + (first + count) * size]
            parts.append((i, slice(x * 128, x * 128 + 128), values, scored(keys, queries(r_ref, x, query_row), biases)))
    done = []
    for i, cols, values, scores in parts:
        old = stat_ref[i * 2 : i * 2 + 1, cols]
        top = jnp.maximum(old, jnp.max(scores, axis=0, keepdims=True))
        exponent = jnp.exp(scores - top)
        share = jnp.exp(old - top)
        total = stat_ref[i * 2 + 1 : i * 2 + 2, cols] * share + jnp.sum(exponent, axis=0, keepdims=True)
        added = sum_ref[i * 128 : i * 128 + 128, cols] * share + dot(values, exponent.astype(BF), (0, 0))
        done.append((i, cols, (added / total).astype(BF), top, total))
    for i, cols, result, top, total in done:
        out_ref[i * 128 : i * 128 + 128, cols] = result
        if i:
            level = top + jnp.log(total)
            high = level.astype(BF)
            left = level - high.astype(F32)
            middle = left.astype(BF)
            low = (left - middle.astype(F32)).astype(BF)
            zeros = jnp.zeros((13, 128), F32)
            pieces = [high.astype(F32), middle.astype(F32), low.astype(F32), zeros]
            out_ref[256:272, cols] = jnp.concatenate(pieces, axis=0).astype(BF)


def project_kernel(ci, zi, xi, g0, g1, g2, g3, own, up5, down6, last, before, after, before2, after2, give_ref, a_ref, keep_w_ref, give_w_ref):
    blocks = [(last, 0, 0, LAST)] + [(ref, 0, 0, step) for ref, step in zip((own, up5, down6), HELD)]
    for ref, step in ((before, -1), (after, 1), (before2, -2), (after2, 2)):
        blocks += [(ref, i * BLOCK, step, offset) for i, offset in enumerate(HELD)]
    for ref, first, step, offset in blocks:
        plane = (zi[0] + step + jnp.where(ci[0] == 0, offset, -offset)) & (NZ - 1)
        rows = pl.ds(pl.multiple_of((plane >> 2) * 160 + (plane & 1) * 80, 80), 80)

        def place(target):
            for head in range(GROUP):
                target[rows, head * HD : head * HD + HD] = ref[first + head * 80 : first + head * 80 + 80]

        pl.when(((plane >> 1) & 1) == ci[0])(lambda: place(keep_w_ref))
        pl.when(((plane >> 1) & 1) != ci[0])(lambda: place(give_w_ref))
    refs = (g0, g1, g2, g3)
    levels = []
    for x in range(NX):
        parts = refs[x][256:272].astype(F32)
        levels.append(parts[0:1] + parts[1:2] + parts[2:3])
    top = jnp.maximum(jnp.maximum(levels[0], levels[1]), jnp.maximum(levels[2], levels[3]))
    shares = [jnp.exp(level - top) for level in levels]
    total = shares[0] + shares[1] + shares[2] + shares[3]
    shared = jnp.zeros((128, 512), F32)
    for x in range(NX):
        head = (xi[0] + x) & (NX - 1)
        a_ref[pl.ds(pl.multiple_of(head * 128, 128), 128)] = refs[x][0:128]
        shared = shared + refs[x][128:256].astype(F32) * (shares[x] / total)
    a_ref[512:640] = shared.astype(BF)
    multiply(give_w_ref, a_ref, give_ref)


def hand_on_kernel(below_w, above_w, attended, below_ref, above_ref):
    del attended
    below_ref[...] = below_w[...]
    above_ref[...] = above_w[...]


def multiply(w_ref, a_ref, out_ref):
    for y in range(4):
        part = dot(w_ref[y * 160 : y * 160 + 160], a_ref[...], (1, 0)).astype(BF)
        for x in range(NX):
            out_ref[x * 4 + y] = part[:, x * 128 : x * 128 + 128]


def keep_kernel(a_ref, w_ref, out_ref):
    multiply(w_ref, a_ref, out_ref)


def final_kernel(r_ref, out_ref, t_ref):
    for x in range(NX):
        total = r_ref[x * 4].astype(F32)
        for y in range(1, 4):
            total = total + r_ref[x * 4 + y].astype(F32)
        t_ref[x * 80 : x * 80 + 80] = total[0:80]
        t_ref[320 + x * 80 : 320 + x * 80 + 80] = total[80:160]
    out_ref[...] = t_ref[...].T.astype(BF)


def call(kernel, out, specs, out_specs=VMEM, scratch=(), limit=LIMIT):
    return pl.pallas_call(
        kernel,
        out_shape=out,
        in_specs=specs,
        out_specs=out_specs,
        scratch_shapes=list(scratch),
        compiler_params=pltpu.CompilerParams(vmem_limit_bytes=limit),
    )


def shape(*dims):
    return jax.ShapeDtypeStruct(dims, BF)


def from_plane(value, step):
    return lax.ppermute(value, "z", [((i + step) % NZ, i) for i in range(NZ)])


def from_either(value, step):
    pairs = [((z + (step, -step)[core]) % NZ * 2 + core, z * 2 + core) for z in range(NZ) for core in range(2)]
    return lax.ppermute(value, ("z", "c"), pairs)


def per_device(query_input, key_input, value_input, query_gain, key_gain, band_lists, out_weight):
    plane = ("x", "y", "c")
    lists = band_lists.reshape(-1)
    zi = lax.axis_index("z").reshape(1)
    xi = lax.axis_index("x").reshape(1)
    packed = call(
        pack_kernel,
        shape(32, CHUNK, HD),
        [ANY] * 5,
        VMEM,
        [
            pltpu.VMEM((QROWS, D), BF),
            pltpu.VMEM((HALF, D), BF),
            pltpu.VMEM((HALF, D), BF),
            pltpu.VMEM((1, D), F32),
            pltpu.VMEM((1, D), F32),
            pltpu.SemaphoreType.DMA((5,)),
        ],
        ALL,
    )(query_input, key_input, value_input, query_gain.reshape(1, -1), key_gain.reshape(1, -1))
    packed, columns = lax.optimization_barrier((packed, out_weight))
    columns = columns.reshape(GROUP, HD, 80).transpose(0, 2, 1).reshape(BLOCK, HD)
    held = [columns] + [from_either(columns, step) for step in HELD[1:]]
    last = from_either(columns, LAST)
    mine = lax.all_to_all(packed, plane, split_axis=0, concat_axis=0, tiled=True)
    up, down, joined = call(
        select_kernel, (shape(SENT, HD), shape(SENT, HD), shape(3 * BLOCK, HD)), [SMEM, SMEM] + [VMEM] * 4 + [ANY], (VMEM,) * 3
    )(lists, zi, mine, *held, last)
    before, after = from_plane(up, -1), from_plane(down, 1)
    sums, stats = call(
        attend_own_kernel,
        (jax.ShapeDtypeStruct((256, 512), F32), jax.ShapeDtypeStruct((8, 512), F32)),
        [SMEM, SMEM, VMEM],
        (VMEM, VMEM),
        [pltpu.VMEM((1024, HD), BF), pltpu.VMEM((1024, HD), BF), pltpu.VMEM((256, HD), BF), pltpu.VMEM((256, HD), BF)],
    )(lists, zi, mine)
    attended = call(attend_rest_kernel, shape(304, 512), [SMEM, SMEM] + [VMEM] * 5)(
        lists, zi, mine, before, after, sums, stats
    )
    above_w, below_w = from_plane(joined, 1), from_plane(joined, -1)
    below_again, above_again = call(
        hand_on_kernel, (shape(3 * BLOCK, HD),) * 2, [VMEM, VMEM, ANY], (VMEM, VMEM)
    )(below_w, above_w, attended)
    below2, above2 = from_plane(below_again, -1), from_plane(above_again, 1)
    gathered = [attended] + [
        lax.ppermute(attended, "x", [((i + step) % NX, i) for i in range(NX)]) for step in (1, 2, 3)
    ]
    ci = lax.axis_index("c").reshape(1)
    give, a, keep_w = call(
        project_kernel,
        (shape(16, 160, 128), shape(640, 512), shape(640, 640)),
        [SMEM, SMEM, SMEM] + [VMEM] * 12,
        (VMEM, VMEM, VMEM),
        [pltpu.VMEM((640, 640), BF)],
    )(ci, zi, xi, *gathered, *held, last, below_w, above_w, below2, above2)
    other = lax.ppermute(give, "c", [(0, 1), (1, 0)])
    keep = call(keep_kernel, shape(16, 160, 128), [VMEM, VMEM])(a, keep_w)
    terms = (keep.astype(F32) + other.astype(F32)).astype(BF)
    summands = lax.all_to_all(terms, ("x", "y"), split_axis=0, concat_axis=0, tiled=True)
    return call(final_kernel, shape(128, 640), [VMEM], VMEM, [pltpu.VMEM((640, 128), F32)])(summands)


def solution(mesh):
    split = Mesh(mesh.devices.reshape(NZ, NX, 4, 2), ("z", "x", "y", "c"))
    rows = P(("z", "x", "y", "c"), None)
    return jax.shard_map(
        per_device,
        mesh=split,
        in_specs=(rows, rows, rows, P(), P(), P(), P(("y", "c"), ("z", "x"))),
        out_specs=P(("z", "x"), ("y", "c")),
        check_vma=False,
    )
```

```python
import jax
import jax.numpy as jnp
from jax import lax
from jax.experimental import pallas as pl
from jax.experimental.pallas import tpu as pltpu
from jax.sharding import Mesh, PartitionSpec as P

HD = 128
D = 5120
HALF = 64
QROWS = 16
NX = 4
NH = 8
NZ = 16
MAXB = 8
GROUP = 5
K0, V0, K5, V5, Q0, Q5, CHUNK = 0, 64, 128, 144, 160, 176, 192
KV = 160
BF = jnp.bfloat16
F32 = jnp.float32
VMEM = pl.BlockSpec(memory_space=pltpu.VMEM)
SMEM = pl.BlockSpec(memory_space=pltpu.SMEM)
ANY = pl.BlockSpec(memory_space=pl.ANY)
LIMIT = 40 * 1024 * 1024
ALL = 60 * 1024 * 1024
HELD = (0, 5, -6)
LAST = -3
BLOCK = 400
SK, SV, SK5, SV5, SENT = 0, 512, 1024, 1152, 1280


def dot(a, b, contract):
    return lax.dot_general(a, b, ((contract[:1], contract[1:]), ((), ())), preferred_element_type=F32)


def pack_kernel(q_hbm, k_hbm, v_hbm, qg_hbm, kg_hbm, out_ref, q_ref, k_ref, v_ref, qg_ref, kg_ref, sems):
    pairs = ((k_hbm, k_ref), (kg_hbm, kg_ref), (q_hbm, q_ref), (qg_hbm, qg_ref), (v_hbm, v_ref))
    copies = [pltpu.make_async_copy(*pair, sems.at[i]) for i, pair in enumerate(pairs)]
    for copy in copies:
        copy.start()
    for copy in copies[:4]:
        copy.wait()

    def inverse(ref):
        wide = ref[...].astype(F32)
        return lax.rsqrt(jnp.mean(wide * wide, axis=-1, keepdims=True) + 1e-06)

    k_inv, q_inv = inverse(k_ref), inverse(q_ref)

    def heads():
        for group in range(NH):
            for at in range(GROUP):
                yield group, at, slice((group * GROUP + at) * HD, (group * GROUP + at + 1) * HD)

    for group, at, cols in heads():
        k = (k_ref[:, cols].astype(F32) * k_inv * kg_ref[:, cols]).astype(BF)
        q = (q_ref[:, cols].astype(F32) * q_inv * qg_ref[:, cols]).astype(BF)
        if at < NX:
            out_ref[at * NH + group, K0 : K0 + HALF] = k
            out_ref[at * NH + group, Q0 : Q0 + QROWS] = q
        else:
            for x in range(NX):
                out_ref[x * NH + group, K5 : K5 + 16] = k[x * 16 : x * 16 + 16]
                out_ref[x * NH + group, Q5 : Q5 + QROWS] = q
    copies[4].wait()
    for group, at, cols in heads():
        if at < NX:
            out_ref[at * NH + group, V0 : V0 + HALF] = v_ref[:, cols]
        else:
            for x in range(NX):
                out_ref[x * NH + group, V5 : V5 + 16] = v_ref[x * 16 : x * 16 + 16, cols]


def listed_of(lists, block, seq, count):
    found = [jnp.int32(-1)] * count
    for m in range(MAXB):
        entry = lists[block * MAXB + m]
        hit = (entry >= 0) & ((entry >> 2) == seq)
        for i in reversed(range(count)):
            free = found[i] < 0
            if i:
                free = free & (found[i - 1] >= 0)
            found[i] = jnp.where(hit & free, entry, found[i])
    return found


def listed_above(lists, z):
    block = jnp.minimum(z + 1, NZ - 1) * 4
    seq = z * 4
    return (
        listed_of(lists, block, seq + 2, 1) + listed_of(lists, block, seq + 3, 2) + listed_of(lists, block + 1, seq + 3, 1)
    )


def listed_below(lists, z):
    block = jnp.maximum(z - 1, 0) * 4
    seq = z * 4
    return (
        listed_of(lists, block + 3, seq + 1, 1) + listed_of(lists, block + 3, seq, 2) + listed_of(lists, block + 2, seq, 1)
    )


def join_kernel(*refs):
    for i, ref in enumerate(refs[:3]):
        refs[-1][i * BLOCK : i * BLOCK + BLOCK] = ref[...]


def select_kernel(lists, zi, r_ref, up_ref, down_ref):
    z = zi[0]
    for blocks, target in ((listed_above(lists, z), up_ref), (listed_below(lists, z), down_ref)):
        for slot, block in enumerate(blocks):
            at = jnp.clip(block - z * 16, 0, 15)
            for half in range(2):
                source, part = r_ref.at[at * 2 + half], slot * 2 + half
                target[SK + part * 64 : SK + part * 64 + 64] = source[K0 : K0 + 64]
                target[SV + part * 64 : SV + part * 64 + 64] = source[V0 : V0 + 64]
                target[SK5 + part * 16 : SK5 + part * 16 + 16] = source[K5 : K5 + 16]
                target[SV5 + part * 16 : SV5 + part * 16 + 16] = source[V5 : V5 + 16]


def queries(r_ref, x, first):
    return r_ref[x * NH : x * NH + NH, first : first + QROWS].reshape(128, HD)


def scored(keys, q, biases):
    raw = dot(keys, q, (1, 1)) * HD**-0.5
    rows = keys.shape[0] // len(biases)
    return jnp.concatenate([raw[i * rows : i * rows + rows] + bias for i, bias in enumerate(biases)], axis=0)


def attend_own_kernel(lists, zi, r_ref, sum_ref, stat_ref, kg, vg, k5g, v5g):
    z = zi[0]
    for x in range(NX):
        biases = []
        for m in range(MAXB):
            entry = lists[(z * 4 + x) * MAXB + m]
            here = (entry >> 4) == z
            at = jnp.where(here, entry - z * 16, 0)
            biases.append(jnp.where(here, 0.0, -jnp.inf))
            for half in range(2):
                row = m * 2 + half
                block = r_ref.at[at * 2 + half]
                kg[row * 64 : row * 64 + 64] = block[K0 : K0 + 64]
                vg[row * 64 : row * 64 + 64] = block[V0 : V0 + 64]
                k5g[row * 16 : row * 16 + 16] = block[K5 : K5 + 16]
                v5g[row * 16 : row * 16 + 16] = block[V5 : V5 + 16]
        cols = slice(x * 128, x * 128 + 128)
        for i, (keys, values, first) in enumerate(((kg, vg, Q0), (k5g, v5g, Q5))):
            scores = scored(keys[...], queries(r_ref, x, first), biases)
            top = jnp.max(scores, axis=0, keepdims=True)
            exponent = jnp.exp(scores - top)
            stat_ref[i * 2 : i * 2 + 1, cols] = top
            stat_ref[i * 2 + 1 : i * 2 + 2, cols] = jnp.sum(exponent, axis=0, keepdims=True)
            sum_ref[i * 128 : i * 128 + 128, cols] = dot(values[...], exponent.astype(BF), (0, 0))


def attend_rest_kernel(lists, zi, r_ref, prev_ref, next_ref, sum_ref, stat_ref, out_ref):
    z = zi[0]
    near = listed_above(lists, z - 1), listed_below(lists, z + 1)
    out_ref[272:] = jnp.zeros((32, 512), BF)
    parts = []
    for x in range(NX):
        ref, side = ((prev_ref, 0), (next_ref, 1))[x // 2]
        first, count = (0, 3) if x in (0, 3) else (3, 1)
        found = near[side][first : first + count]
        inside = (z > 0) if side == 0 else (z < NZ - 1)
        biases = [jnp.where((block >= 0) & inside, 0.0, -jnp.inf) for block in found]
        for i, (key_row, value_row, size, query_row) in enumerate(((SK, SV, 128, Q0), (SK5, SV5, 32, Q5))):
            keys = ref[key_row + first * size : key_row + (first + count) * size]
            values = ref[value_row + first * size : value_row + (first + count) * size]
            parts.append((i, slice(x * 128, x * 128 + 128), values, scored(keys, queries(r_ref, x, query_row), biases)))
    done = []
    for i, cols, values, scores in parts:
        old = stat_ref[i * 2 : i * 2 + 1, cols]
        top = jnp.maximum(old, jnp.max(scores, axis=0, keepdims=True))
        exponent = jnp.exp(scores - top)
        share = jnp.exp(old - top)
        total = stat_ref[i * 2 + 1 : i * 2 + 2, cols] * share + jnp.sum(exponent, axis=0, keepdims=True)
        added = sum_ref[i * 128 : i * 128 + 128, cols] * share + dot(values, exponent.astype(BF), (0, 0))
        done.append((i, cols, (added / total).astype(BF), top, total))
    for i, cols, result, top, total in done:
        out_ref[i * 128 : i * 128 + 128, cols] = result
        if i:
            level = top + jnp.log(total)
            high = level.astype(BF)
            left = level - high.astype(F32)
            middle = left.astype(BF)
            low = (left - middle.astype(F32)).astype(BF)
            zeros = jnp.zeros((13, 128), F32)
            pieces = [high.astype(F32), middle.astype(F32), low.astype(F32), zeros]
            out_ref[256:272, cols] = jnp.concatenate(pieces, axis=0).astype(BF)


def project_kernel(ci, zi, xi, g0, g1, g2, g3, own, up5, down6, last, before, after, before2, after2, give_ref, a_ref, keep_w_ref, give_w_ref):
    blocks = [(last, 0, 0, LAST)] + [(ref, 0, 0, step) for ref, step in zip((own, up5, down6), HELD)]
    for ref, step in ((before, -1), (after, 1), (before2, -2), (after2, 2)):
        blocks += [(ref, i * BLOCK, step, offset) for i, offset in enumerate(HELD)]
    for ref, first, step, offset in blocks:
        plane = (zi[0] + step + jnp.where(ci[0] == 0, offset, -offset)) & (NZ - 1)
        rows = pl.ds(pl.multiple_of((plane >> 2) * 160 + (plane & 1) * 80, 80), 80)

        def place(target):
            for head in range(GROUP):
                target[rows, head * HD : head * HD + HD] = ref[first + head * 80 : first + head * 80 + 80]

        pl.when(((plane >> 1) & 1) == ci[0])(lambda: place(keep_w_ref))
        pl.when(((plane >> 1) & 1) != ci[0])(lambda: place(give_w_ref))
    refs = (g0, g1, g2, g3)
    levels = []
    for x in range(NX):
        parts = refs[x][256:272].astype(F32)
        levels.append(parts[0:1] + parts[1:2] + parts[2:3])
    top = jnp.maximum(jnp.maximum(levels[0], levels[1]), jnp.maximum(levels[2], levels[3]))
    shares = [jnp.exp(level - top) for level in levels]
    total = shares[0] + shares[1] + shares[2] + shares[3]
    shared = jnp.zeros((128, 512), F32)
    for x in range(NX):
        head = (xi[0] + x) & (NX - 1)
        a_ref[pl.ds(pl.multiple_of(head * 128, 128), 128)] = refs[x][0:128]
        shared = shared + refs[x][128:256].astype(F32) * (shares[x] / total)
    a_ref[512:640] = shared.astype(BF)
    multiply(give_w_ref, a_ref, give_ref)


def hand_on_kernel(below_w, above_w, attended, below_ref, above_ref):
    del attended
    below_ref[...] = below_w[...]
    above_ref[...] = above_w[...]


def multiply(w_ref, a_ref, out_ref):
    for y in range(4):
        part = dot(w_ref[y * 160 : y * 160 + 160], a_ref[...], (1, 0)).astype(BF)
        for x in range(NX):
            out_ref[x * 4 + y] = part[:, x * 128 : x * 128 + 128]


def keep_kernel(a_ref, w_ref, out_ref):
    multiply(w_ref, a_ref, out_ref)


def final_kernel(r_ref, out_ref, t_ref):
    for x in range(NX):
        total = r_ref[x * 4].astype(F32)
        for y in range(1, 4):
            total = total + r_ref[x * 4 + y].astype(F32)
        t_ref[x * 80 : x * 80 + 80] = total[0:80]
        t_ref[320 + x * 80 : 320 + x * 80 + 80] = total[80:160]
    out_ref[...] = t_ref[...].T.astype(BF)


def call(kernel, out, specs, out_specs=VMEM, scratch=(), limit=LIMIT):
    return pl.pallas_call(
        kernel,
        out_shape=out,
        in_specs=specs,
        out_specs=out_specs,
        scratch_shapes=list(scratch),
        compiler_params=pltpu.CompilerParams(vmem_limit_bytes=limit),
    )


def shape(*dims):
    return jax.ShapeDtypeStruct(dims, BF)


def from_plane(value, step):
    return lax.ppermute(value, "z", [((i + step) % NZ, i) for i in range(NZ)])


def from_either(value, step):
    pairs = [((z + (step, -step)[core]) % NZ * 2 + core, z * 2 + core) for z in range(NZ) for core in range(2)]
    return lax.ppermute(value, ("z", "c"), pairs)


def per_device(query_input, key_input, value_input, query_gain, key_gain, band_lists, out_weight):
    plane = ("x", "y", "c")
    lists = band_lists.reshape(-1)
    zi = lax.axis_index("z").reshape(1)
    xi = lax.axis_index("x").reshape(1)
    packed = call(
        pack_kernel,
        shape(32, CHUNK, HD),
        [ANY] * 5,
        VMEM,
        [
            pltpu.VMEM((QROWS, D), BF),
            pltpu.VMEM((HALF, D), BF),
            pltpu.VMEM((HALF, D), BF),
            pltpu.VMEM((1, D), F32),
            pltpu.VMEM((1, D), F32),
            pltpu.SemaphoreType.DMA((5,)),
        ],
        ALL,
    )(query_input, key_input, value_input, query_gain.reshape(1, -1), key_gain.reshape(1, -1))
    packed, columns = lax.optimization_barrier((packed, out_weight))
    columns = columns.reshape(GROUP, HD, 80).transpose(0, 2, 1).reshape(BLOCK, HD)
    held = [columns] + [from_either(columns, step) for step in HELD[1:]]
    last = from_either(columns, LAST)
    mine = lax.all_to_all(packed, plane, split_axis=0, concat_axis=0, tiled=True)
    up, down = call(select_kernel, (shape(SENT, HD),) * 2, [SMEM, SMEM, VMEM], (VMEM, VMEM))(lists, zi, mine)
    joined = call(join_kernel, shape(3 * BLOCK, HD), [VMEM] * 3 + [ANY])(*held, last)
    before, after = from_plane(up, -1), from_plane(down, 1)
    sums, stats = call(
        attend_own_kernel,
        (jax.ShapeDtypeStruct((256, 512), F32), jax.ShapeDtypeStruct((8, 512), F32)),
        [SMEM, SMEM, VMEM],
        (VMEM, VMEM),
        [pltpu.VMEM((1024, HD), BF), pltpu.VMEM((1024, HD), BF), pltpu.VMEM((256, HD), BF), pltpu.VMEM((256, HD), BF)],
    )(lists, zi, mine)
    attended = call(attend_rest_kernel, shape(304, 512), [SMEM, SMEM] + [VMEM] * 5)(
        lists, zi, mine, before, after, sums, stats
    )
    above_w, below_w = from_plane(joined, 1), from_plane(joined, -1)
    below_again, above_again = call(
        hand_on_kernel, (shape(3 * BLOCK, HD),) * 2, [VMEM, VMEM, ANY], (VMEM, VMEM)
    )(below_w, above_w, attended)
    below2, above2 = from_plane(below_again, -1), from_plane(above_again, 1)
    gathered = [attended] + [
        lax.ppermute(attended, "x", [((i + step) % NX, i) for i in range(NX)]) for step in (1, 2, 3)
    ]
    ci = lax.axis_index("c").reshape(1)
    give, a, keep_w = call(
        project_kernel,
        (shape(16, 160, 128), shape(640, 512), shape(640, 640)),
        [SMEM, SMEM, SMEM] + [VMEM] * 12,
        (VMEM, VMEM, VMEM),
        [pltpu.VMEM((640, 640), BF)],
    )(ci, zi, xi, *gathered, *held, last, below_w, above_w, below2, above2)
    other = lax.ppermute(give, "c", [(0, 1), (1, 0)])
    keep = call(keep_kernel, shape(16, 160, 128), [VMEM, VMEM])(a, keep_w)
    terms = (keep.astype(F32) + other.astype(F32)).astype(BF)
    summands = lax.all_to_all(terms, ("x", "y"), split_axis=0, concat_axis=0, tiled=True)
    return call(final_kernel, shape(128, 640), [VMEM], VMEM, [pltpu.VMEM((640, 128), F32)])(summands)


def solution(mesh):
    split = Mesh(mesh.devices.reshape(NZ, NX, 4, 2), ("z", "x", "y", "c"))
    rows = P(("z", "x", "y", "c"), None)
    return jax.shard_map(
        per_device,
        mesh=split,
        in_specs=(rows, rows, rows, P(), P(), P(), P(("y", "c"), ("z", "x"))),
        out_specs=P(("z", "x"), ("y", "c")),
        check_vma=False,
    )
```

```python
import jax
import jax.numpy as jnp
from jax import lax
from jax.experimental import pallas as pl
from jax.experimental.pallas import tpu as pltpu
from jax.sharding import Mesh, PartitionSpec as P

HD = 128
D = 5120
HALF = 64
QROWS = 16
NX = 4
NH = 8
NZ = 16
MAXB = 8
GROUP = 5
K0, V0, K5, V5, Q0, Q5, CHUNK = 0, 64, 128, 144, 160, 176, 192
KV = 160
BF = jnp.bfloat16
F32 = jnp.float32
VMEM = pl.BlockSpec(memory_space=pltpu.VMEM)
SMEM = pl.BlockSpec(memory_space=pltpu.SMEM)
ANY = pl.BlockSpec(memory_space=pl.ANY)
LIMIT = 40 * 1024 * 1024
ALL = 60 * 1024 * 1024
HELD = (0, 5, -6)
LAST = -3
BLOCK = 400
SK, SV, SK5, SV5, SENT = 0, 512, 1024, 1152, 1280


def dot(a, b, contract):
    return lax.dot_general(a, b, ((contract[:1], contract[1:]), ((), ())), preferred_element_type=F32)


def pack_kernel(q_hbm, k_hbm, v_hbm, qg_hbm, kg_hbm, out_hbm, q_ref, k_ref, v_ref, qg_ref, kg_ref, out_ref, sems, out_sems):
    pairs = ((k_hbm, k_ref), (kg_hbm, kg_ref), (q_hbm, q_ref), (qg_hbm, qg_ref), (v_hbm, v_ref))
    copies = [pltpu.make_async_copy(*pair, sems.at[i]) for i, pair in enumerate(pairs)]
    for copy in copies:
        copy.start()
    for copy in copies[:4]:
        copy.wait()

    def inverse(ref):
        wide = ref[...].astype(F32)
        return lax.rsqrt(jnp.mean(wide * wide, axis=-1, keepdims=True) + 1e-06)

    k_inv, q_inv = inverse(k_ref), inverse(q_ref)
    copies[4].wait()
    leaving = []
    for at in (4, 0, 1, 2, 3):
        for group in range(NH):
            cols = slice((group * GROUP + at) * HD, (group * GROUP + at + 1) * HD)
            k = (k_ref[:, cols].astype(F32) * k_inv * kg_ref[:, cols]).astype(BF)
            q = (q_ref[:, cols].astype(F32) * q_inv * qg_ref[:, cols]).astype(BF)
            v = v_ref[:, cols]
            if at < NX:
                chunk = at * NH + group
                out_ref[chunk, K0 : K0 + HALF] = k
                out_ref[chunk, V0 : V0 + HALF] = v
                out_ref[chunk, Q0 : Q0 + QROWS] = q
            else:
                for x in range(NX):
                    chunk = x * NH + group
                    rows = slice(x * 16, x * 16 + 16)
                    out_ref[chunk, K5 : K5 + 16] = k[rows]
                    out_ref[chunk, V5 : V5 + 16] = v[rows]
                    out_ref[chunk, Q5 : Q5 + QROWS] = q
        if at < NX:
            part = pl.ds(at * NH, NH)
            leaving.append(pltpu.make_async_copy(out_ref.at[part], out_hbm.at[part], out_sems.at[at]))
            leaving[-1].start()
    for copy in leaving:
        copy.wait()


def listed_of(lists, block, seq, count):
    found = [jnp.int32(-1)] * count
    for m in range(MAXB):
        entry = lists[block * MAXB + m]
        hit = (entry >= 0) & ((entry >> 2) == seq)
        for i in reversed(range(count)):
            free = found[i] < 0
            if i:
                free = free & (found[i - 1] >= 0)
            found[i] = jnp.where(hit & free, entry, found[i])
    return found


def listed_above(lists, z):
    block = jnp.minimum(z + 1, NZ - 1) * 4
    seq = z * 4
    return (
        listed_of(lists, block, seq + 2, 1) + listed_of(lists, block, seq + 3, 2) + listed_of(lists, block + 1, seq + 3, 1)
    )


def listed_below(lists, z):
    block = jnp.maximum(z - 1, 0) * 4
    seq = z * 4
    return (
        listed_of(lists, block + 3, seq + 1, 1) + listed_of(lists, block + 3, seq, 2) + listed_of(lists, block + 2, seq, 1)
    )


def join_kernel(*refs):
    for i, ref in enumerate(refs[:3]):
        refs[-1][i * BLOCK : i * BLOCK + BLOCK] = ref[...]


def select_kernel(lists, zi, r_ref, up_ref, down_ref):
    z = zi[0]
    for blocks, target in ((listed_above(lists, z), up_ref), (listed_below(lists, z), down_ref)):
        for slot, block in enumerate(blocks):
            at = jnp.clip(block - z * 16, 0, 15)
            for half in range(2):
                source, part = r_ref.at[at * 2 + half], slot * 2 + half
                target[SK + part * 64 : SK + part * 64 + 64] = source[K0 : K0 + 64]
                target[SV + part * 64 : SV + part * 64 + 64] = source[V0 : V0 + 64]
                target[SK5 + part * 16 : SK5 + part * 16 + 16] = source[K5 : K5 + 16]
                target[SV5 + part * 16 : SV5 + part * 16 + 16] = source[V5 : V5 + 16]


def queries(r_ref, x, first):
    return r_ref[x * NH : x * NH + NH, first : first + QROWS].reshape(128, HD)


def scored(keys, q, biases):
    raw = dot(keys, q, (1, 1)) * HD**-0.5
    rows = keys.shape[0] // len(biases)
    return jnp.concatenate([raw[i * rows : i * rows + rows] + bias for i, bias in enumerate(biases)], axis=0)


def attend_own_kernel(lists, zi, r_ref, sum_ref, stat_ref, kg, vg, k5g, v5g):
    z = zi[0]
    for x in range(NX):
        biases = []
        for m in range(MAXB):
            entry = lists[(z * 4 + x) * MAXB + m]
            here = (entry >> 4) == z
            at = jnp.where(here, entry - z * 16, 0)
            biases.append(jnp.where(here, 0.0, -jnp.inf))
            for half in range(2):
                row = m * 2 + half
                block = r_ref.at[at * 2 + half]
                kg[row * 64 : row * 64 + 64] = block[K0 : K0 + 64]
                vg[row * 64 : row * 64 + 64] = block[V0 : V0 + 64]
                k5g[row * 16 : row * 16 + 16] = block[K5 : K5 + 16]
                v5g[row * 16 : row * 16 + 16] = block[V5 : V5 + 16]
        cols = slice(x * 128, x * 128 + 128)
        for i, (keys, values, first) in enumerate(((kg, vg, Q0), (k5g, v5g, Q5))):
            scores = scored(keys[...], queries(r_ref, x, first), biases)
            top = jnp.max(scores, axis=0, keepdims=True)
            exponent = jnp.exp(scores - top)
            stat_ref[i * 2 : i * 2 + 1, cols] = top
            stat_ref[i * 2 + 1 : i * 2 + 2, cols] = jnp.sum(exponent, axis=0, keepdims=True)
            sum_ref[i * 128 : i * 128 + 128, cols] = dot(values[...], exponent.astype(BF), (0, 0))


def attend_rest_kernel(lists, zi, r_ref, prev_ref, next_ref, sum_ref, stat_ref, out_ref):
    z = zi[0]
    near = listed_above(lists, z - 1), listed_below(lists, z + 1)
    out_ref[272:] = jnp.zeros((32, 512), BF)
    parts = []
    for x in range(NX):
        ref, side = ((prev_ref, 0), (next_ref, 1))[x // 2]
        first, count = (0, 3) if x in (0, 3) else (3, 1)
        found = near[side][first : first + count]
        inside = (z > 0) if side == 0 else (z < NZ - 1)
        biases = [jnp.where((block >= 0) & inside, 0.0, -jnp.inf) for block in found]
        for i, (key_row, value_row, size, query_row) in enumerate(((SK, SV, 128, Q0), (SK5, SV5, 32, Q5))):
            keys = ref[key_row + first * size : key_row + (first + count) * size]
            values = ref[value_row + first * size : value_row + (first + count) * size]
            parts.append((i, slice(x * 128, x * 128 + 128), values, scored(keys, queries(r_ref, x, query_row), biases)))
    done = []
    for i, cols, values, scores in parts:
        old = stat_ref[i * 2 : i * 2 + 1, cols]
        top = jnp.maximum(old, jnp.max(scores, axis=0, keepdims=True))
        exponent = jnp.exp(scores - top)
        share = jnp.exp(old - top)
        total = stat_ref[i * 2 + 1 : i * 2 + 2, cols] * share + jnp.sum(exponent, axis=0, keepdims=True)
        added = sum_ref[i * 128 : i * 128 + 128, cols] * share + dot(values, exponent.astype(BF), (0, 0))
        done.append((i, cols, (added / total).astype(BF), top, total))
    for i, cols, result, top, total in done:
        out_ref[i * 128 : i * 128 + 128, cols] = result
        if i:
            level = top + jnp.log(total)
            high = level.astype(BF)
            left = level - high.astype(F32)
            middle = left.astype(BF)
            low = (left - middle.astype(F32)).astype(BF)
            zeros = jnp.zeros((13, 128), F32)
            pieces = [high.astype(F32), middle.astype(F32), low.astype(F32), zeros]
            out_ref[256:272, cols] = jnp.concatenate(pieces, axis=0).astype(BF)


def project_kernel(ci, zi, xi, g0, g1, g2, g3, own, up5, down6, last, before, after, before2, after2, give_ref, a_ref, keep_w_ref, give_w_ref):
    blocks = [(last, 0, 0, LAST)] + [(ref, 0, 0, step) for ref, step in zip((own, up5, down6), HELD)]
    for ref, step in ((before, -1), (after, 1), (before2, -2), (after2, 2)):
        blocks += [(ref, i * BLOCK, step, offset) for i, offset in enumerate(HELD)]
    for ref, first, step, offset in blocks:
        plane = (zi[0] + step + jnp.where(ci[0] == 0, offset, -offset)) & (NZ - 1)
        rows = pl.ds(pl.multiple_of((plane >> 2) * 160 + (plane & 1) * 80, 80), 80)

        def place(target):
            for head in range(GROUP):
                target[rows, head * HD : head * HD + HD] = ref[first + head * 80 : first + head * 80 + 80]

        pl.when(((plane >> 1) & 1) == ci[0])(lambda: place(keep_w_ref))
        pl.when(((plane >> 1) & 1) != ci[0])(lambda: place(give_w_ref))
    refs = (g0, g1, g2, g3)
    levels = []
    for x in range(NX):
        parts = refs[x][256:272].astype(F32)
        levels.append(parts[0:1] + parts[1:2] + parts[2:3])
    top = jnp.maximum(jnp.maximum(levels[0], levels[1]), jnp.maximum(levels[2], levels[3]))
    shares = [jnp.exp(level - top) for level in levels]
    total = shares[0] + shares[1] + shares[2] + shares[3]
    shared = jnp.zeros((128, 512), F32)
    for x in range(NX):
        head = (xi[0] + x) & (NX - 1)
        a_ref[pl.ds(pl.multiple_of(head * 128, 128), 128)] = refs[x][0:128]
        shared = shared + refs[x][128:256].astype(F32) * (shares[x] / total)
    a_ref[512:640] = shared.astype(BF)
    multiply(give_w_ref, a_ref, give_ref)


def hand_on_kernel(below_w, above_w, attended, below_ref, above_ref):
    del below_w, above_w, attended, below_ref, above_ref


def multiply(w_ref, a_ref, out_ref):
    for y in range(4):
        part = dot(w_ref[y * 160 : y * 160 + 160], a_ref[...], (1, 0)).astype(BF)
        for x in range(NX):
            out_ref[x * 4 + y] = part[:, x * 128 : x * 128 + 128]


def keep_kernel(a_ref, w_ref, out_ref):
    multiply(w_ref, a_ref, out_ref)


def final_kernel(r_ref, out_ref, t_ref):
    for x in range(NX):
        total = r_ref[x * 4].astype(F32)
        for y in range(1, 4):
            total = total + r_ref[x * 4 + y].astype(F32)
        t_ref[x * 80 : x * 80 + 80] = total[0:80]
        t_ref[320 + x * 80 : 320 + x * 80 + 80] = total[80:160]
    out_ref[...] = t_ref[...].T.astype(BF)


def call(kernel, out, specs, out_specs=VMEM, scratch=(), limit=LIMIT, aliases=None):
    return pl.pallas_call(
        kernel,
        out_shape=out,
        in_specs=specs,
        out_specs=out_specs,
        scratch_shapes=list(scratch),
        input_output_aliases=aliases or {},
        compiler_params=pltpu.CompilerParams(vmem_limit_bytes=limit),
    )


def shape(*dims):
    return jax.ShapeDtypeStruct(dims, BF)


def from_plane(value, step):
    return lax.ppermute(value, "z", [((i + step) % NZ, i) for i in range(NZ)])


def from_either(value, step):
    pairs = [((z + (step, -step)[core]) % NZ * 2 + core, z * 2 + core) for z in range(NZ) for core in range(2)]
    return lax.ppermute(value, ("z", "c"), pairs)


def per_device(query_input, key_input, value_input, query_gain, key_gain, band_lists, out_weight):
    plane = ("x", "y", "c")
    lists = band_lists.reshape(-1)
    zi = lax.axis_index("z").reshape(1)
    xi = lax.axis_index("x").reshape(1)
    packed = call(
        pack_kernel,
        shape(32, CHUNK, HD),
        [ANY] * 5,
        ANY,
        [
            pltpu.VMEM((QROWS, D), BF),
            pltpu.VMEM((HALF, D), BF),
            pltpu.VMEM((HALF, D), BF),
            pltpu.VMEM((1, D), F32),
            pltpu.VMEM((1, D), F32),
            pltpu.VMEM((32, CHUNK, HD), BF),
            pltpu.SemaphoreType.DMA((5,)),
            pltpu.SemaphoreType.DMA((NX,)),
        ],
        ALL,
    )(query_input, key_input, value_input, query_gain.reshape(1, -1), key_gain.reshape(1, -1))
    packed, columns = lax.optimization_barrier((packed, out_weight))
    columns = columns.reshape(GROUP, HD, 80).transpose(0, 2, 1).reshape(BLOCK, HD)
    held = [columns] + [from_either(columns, step) for step in HELD[1:]]
    last = from_either(columns, LAST)
    mine = lax.all_to_all(packed, plane, split_axis=0, concat_axis=0, tiled=True)
    up, down = call(select_kernel, (shape(SENT, HD),) * 2, [SMEM, SMEM, VMEM], (VMEM, VMEM))(lists, zi, mine)
    before, after = from_plane(up, -1), from_plane(down, 1)
    sums, stats = call(
        attend_own_kernel,
        (jax.ShapeDtypeStruct((256, 512), F32), jax.ShapeDtypeStruct((8, 512), F32)),
        [SMEM, SMEM, VMEM],
        (VMEM, VMEM),
        [pltpu.VMEM((1024, HD), BF), pltpu.VMEM((1024, HD), BF), pltpu.VMEM((256, HD), BF), pltpu.VMEM((256, HD), BF)],
    )(lists, zi, mine)
    joined = call(join_kernel, shape(3 * BLOCK, HD), [VMEM] * 3 + [ANY] * 2)(*held, last, stats)
    attended = call(attend_rest_kernel, shape(304, 512), [SMEM, SMEM] + [VMEM] * 5)(
        lists, zi, mine, before, after, sums, stats
    )
    above_w, below_w = from_plane(joined, 1), from_plane(joined, -1)
    below_again, above_again = call(
        hand_on_kernel, (shape(3 * BLOCK, HD),) * 2, [ANY] * 3, (ANY, ANY), aliases={0: 0, 1: 1}
    )(below_w, above_w, attended)
    below2, above2 = from_plane(below_again, -1), from_plane(above_again, 1)
    gathered = [attended] + [
        lax.ppermute(attended, "x", [((i + step) % NX, i) for i in range(NX)]) for step in (1, 2, 3)
    ]
    ci = lax.axis_index("c").reshape(1)
    give, a, keep_w = call(
        project_kernel,
        (shape(16, 160, 128), shape(640, 512), shape(640, 640)),
        [SMEM, SMEM, SMEM] + [VMEM] * 12,
        (VMEM, VMEM, VMEM),
        [pltpu.VMEM((640, 640), BF)],
    )(ci, zi, xi, *gathered, *held, last, below_again, above_again, below2, above2)
    other = lax.ppermute(give, "c", [(0, 1), (1, 0)])
    keep = call(keep_kernel, shape(16, 160, 128), [VMEM, VMEM])(a, keep_w)
    terms = (keep.astype(F32) + other.astype(F32)).astype(BF)
    summands = lax.all_to_all(terms, ("x", "y"), split_axis=0, concat_axis=0, tiled=True)
    return call(final_kernel, shape(128, 640), [VMEM], VMEM, [pltpu.VMEM((640, 128), F32)])(summands)


def solution(mesh):
    split = Mesh(mesh.devices.reshape(NZ, NX, 4, 2), ("z", "x", "y", "c"))
    rows = P(("z", "x", "y", "c"), None)
    return jax.shard_map(
        per_device,
        mesh=split,
        in_specs=(rows, rows, rows, P(), P(), P(), P(("y", "c"), ("z", "x"))),
        out_specs=P(("z", "x"), ("y", "c")),
        check_vma=False,
    )
```

```python
import jax
import jax.numpy as jnp
from jax import lax
from jax.experimental import pallas as pl
from jax.experimental.pallas import tpu as pltpu
from jax.sharding import Mesh, PartitionSpec as P

HD = 128
D = 5120
HALF = 64
QROWS = 16
NX = 4
NH = 8
NZ = 16
MAXB = 8
GROUP = 5
K0, V0, K5, V5, Q0, Q5, CHUNK = 0, 64, 128, 144, 160, 176, 192
KV = 160
BF = jnp.bfloat16
F32 = jnp.float32
VMEM = pl.BlockSpec(memory_space=pltpu.VMEM)
SMEM = pl.BlockSpec(memory_space=pltpu.SMEM)
ANY = pl.BlockSpec(memory_space=pl.ANY)
LIMIT = 40 * 1024 * 1024
ALL = 60 * 1024 * 1024
HELD = (0, 5, -6)
LAST = -3
BLOCK = 400
SK, SV, SK5, SV5, SENT = 0, 512, 1024, 1152, 1280


def dot(a, b, contract):
    return lax.dot_general(a, b, ((contract[:1], contract[1:]), ((), ())), preferred_element_type=F32)


def pack_kernel(q_hbm, k_hbm, v_hbm, qg_hbm, kg_hbm, out_hbm, q_ref, k_ref, v_ref, qg_ref, kg_ref, out_ref, sems, out_sems):
    pairs = ((k_hbm, k_ref), (kg_hbm, kg_ref), (q_hbm, q_ref), (qg_hbm, qg_ref), (v_hbm, v_ref))
    copies = [pltpu.make_async_copy(*pair, sems.at[i]) for i, pair in enumerate(pairs)]
    for copy in copies:
        copy.start()
    for copy in copies[:4]:
        copy.wait()

    def inverse(ref):
        wide = ref[...].astype(F32)
        return lax.rsqrt(jnp.mean(wide * wide, axis=-1, keepdims=True) + 1e-06)

    k_inv, q_inv = inverse(k_ref), inverse(q_ref)
    copies[4].wait()
    leaving = []
    for at in (4, 0, 1, 2, 3):
        for group in range(NH):
            cols = slice((group * GROUP + at) * HD, (group * GROUP + at + 1) * HD)
            k = (k_ref[:, cols].astype(F32) * k_inv * kg_ref[:, cols]).astype(BF)
            q = (q_ref[:, cols].astype(F32) * q_inv * qg_ref[:, cols]).astype(BF)
            v = v_ref[:, cols]
            if at < NX:
                chunk = at * NH + group
                out_ref[chunk, K0 : K0 + HALF] = k
                out_ref[chunk, V0 : V0 + HALF] = v
                out_ref[chunk, Q0 : Q0 + QROWS] = q
            else:
                for x in range(NX):
                    chunk = x * NH + group
                    rows = slice(x * 16, x * 16 + 16)
                    out_ref[chunk, K5 : K5 + 16] = k[rows]
                    out_ref[chunk, V5 : V5 + 16] = v[rows]
                    out_ref[chunk, Q5 : Q5 + QROWS] = q
        if at < NX:
            part = pl.ds(at * NH, NH)
            leaving.append(pltpu.make_async_copy(out_ref.at[part], out_hbm.at[part], out_sems.at[at]))
            leaving[-1].start()
    for copy in leaving:
        copy.wait()


def listed_of(lists, block, seq, count):
    found = [jnp.int32(-1)] * count
    for m in range(MAXB):
        entry = lists[block * MAXB + m]
        hit = (entry >= 0) & ((entry >> 2) == seq)
        for i in reversed(range(count)):
            free = found[i] < 0
            if i:
                free = free & (found[i - 1] >= 0)
            found[i] = jnp.where(hit & free, entry, found[i])
    return found


def listed_above(lists, z):
    block = jnp.minimum(z + 1, NZ - 1) * 4
    seq = z * 4
    return (
        listed_of(lists, block, seq + 2, 1) + listed_of(lists, block, seq + 3, 2) + listed_of(lists, block + 1, seq + 3, 1)
    )


def listed_below(lists, z):
    block = jnp.maximum(z - 1, 0) * 4
    seq = z * 4
    return (
        listed_of(lists, block + 3, seq + 1, 1) + listed_of(lists, block + 3, seq, 2) + listed_of(lists, block + 2, seq, 1)
    )


def join_kernel(*refs):
    for i, ref in enumerate(refs[:3]):
        refs[-1][i * BLOCK : i * BLOCK + BLOCK] = ref[...]


def select_kernel(lists, zi, r_ref, up_ref, down_ref):
    z = zi[0]
    for blocks, target in ((listed_above(lists, z), up_ref), (listed_below(lists, z), down_ref)):
        for slot, block in enumerate(blocks):
            at = jnp.clip(block - z * 16, 0, 15)
            for half in range(2):
                source, part = r_ref.at[at * 2 + half], slot * 2 + half
                target[SK + part * 64 : SK + part * 64 + 64] = source[K0 : K0 + 64]
                target[SV + part * 64 : SV + part * 64 + 64] = source[V0 : V0 + 64]
                target[SK5 + part * 16 : SK5 + part * 16 + 16] = source[K5 : K5 + 16]
                target[SV5 + part * 16 : SV5 + part * 16 + 16] = source[V5 : V5 + 16]


def queries(r_ref, x, first):
    return r_ref[x * NH : x * NH + NH, first : first + QROWS].reshape(128, HD)


def scored(keys, q, biases):
    raw = dot(keys, q, (1, 1)) * HD**-0.5
    rows = keys.shape[0] // len(biases)
    return jnp.concatenate([raw[i * rows : i * rows + rows] + bias for i, bias in enumerate(biases)], axis=0)


def attend_own_kernel(lists, zi, r_ref, sum_ref, stat_ref, kg, vg, k5g, v5g):
    z = zi[0]
    for x in range(NX):
        biases = []
        for m in range(MAXB):
            entry = lists[(z * 4 + x) * MAXB + m]
            here = (entry >> 4) == z
            at = jnp.where(here, entry - z * 16, 0)
            biases.append(jnp.where(here, 0.0, -jnp.inf))
            for half in range(2):
                row = m * 2 + half
                block = r_ref.at[at * 2 + half]
                kg[row * 64 : row * 64 + 64] = block[K0 : K0 + 64]
                vg[row * 64 : row * 64 + 64] = block[V0 : V0 + 64]
                k5g[row * 16 : row * 16 + 16] = block[K5 : K5 + 16]
                v5g[row * 16 : row * 16 + 16] = block[V5 : V5 + 16]
        cols = slice(x * 128, x * 128 + 128)
        for i, (keys, values, first) in enumerate(((kg, vg, Q0), (k5g, v5g, Q5))):
            scores = scored(keys[...], queries(r_ref, x, first), biases)
            top = jnp.max(scores, axis=0, keepdims=True)
            exponent = jnp.exp(scores - top)
            stat_ref[i * 2 : i * 2 + 1, cols] = top
            stat_ref[i * 2 + 1 : i * 2 + 2, cols] = jnp.sum(exponent, axis=0, keepdims=True)
            sum_ref[i * 128 : i * 128 + 128, cols] = dot(values[...], exponent.astype(BF), (0, 0))


def attend_rest_kernel(lists, zi, r_ref, prev_ref, next_ref, sum_ref, stat_ref, out_ref):
    z = zi[0]
    near = listed_above(lists, z - 1), listed_below(lists, z + 1)
    out_ref[272:] = jnp.zeros((32, 512), BF)
    parts = []
    for x in range(NX):
        ref, side = ((prev_ref, 0), (next_ref, 1))[x // 2]
        first, count = (0, 3) if x in (0, 3) else (3, 1)
        found = near[side][first : first + count]
        inside = (z > 0) if side == 0 else (z < NZ - 1)
        biases = [jnp.where((block >= 0) & inside, 0.0, -jnp.inf) for block in found]
        for i, (key_row, value_row, size, query_row) in enumerate(((SK, SV, 128, Q0), (SK5, SV5, 32, Q5))):
            keys = ref[key_row + first * size : key_row + (first + count) * size]
            values = ref[value_row + first * size : value_row + (first + count) * size]
            parts.append((i, slice(x * 128, x * 128 + 128), values, scored(keys, queries(r_ref, x, query_row), biases)))
    done = []
    for i, cols, values, scores in parts:
        old = stat_ref[i * 2 : i * 2 + 1, cols]
        top = jnp.maximum(old, jnp.max(scores, axis=0, keepdims=True))
        exponent = jnp.exp(scores - top)
        share = jnp.exp(old - top)
        total = stat_ref[i * 2 + 1 : i * 2 + 2, cols] * share + jnp.sum(exponent, axis=0, keepdims=True)
        added = sum_ref[i * 128 : i * 128 + 128, cols] * share + dot(values, exponent.astype(BF), (0, 0))
        done.append((i, cols, (added / total).astype(BF), top, total))
    for i, cols, result, top, total in done:
        out_ref[i * 128 : i * 128 + 128, cols] = result
        if i:
            level = top + jnp.log(total)
            high = level.astype(BF)
            left = level - high.astype(F32)
            middle = left.astype(BF)
            low = (left - middle.astype(F32)).astype(BF)
            zeros = jnp.zeros((13, 128), F32)
            pieces = [high.astype(F32), middle.astype(F32), low.astype(F32), zeros]
            out_ref[256:272, cols] = jnp.concatenate(pieces, axis=0).astype(BF)


def project_kernel(ci, zi, xi, g0, g1, g2, g3, own, up5, down6, last, before, after, before2, after2, give_ref, a_ref, keep_w_ref, give_w_ref):
    blocks = [(last, 0, 0, LAST)] + [(ref, 0, 0, step) for ref, step in zip((own, up5, down6), HELD)]
    for ref, step in ((before, -1), (after, 1), (before2, -2), (after2, 2)):
        blocks += [(ref, i * BLOCK, step, offset) for i, offset in enumerate(HELD)]
    for ref, first, step, offset in blocks:
        plane = (zi[0] + step + jnp.where(ci[0] == 0, offset, -offset)) & (NZ - 1)
        rows = pl.ds(pl.multiple_of((plane >> 2) * 160 + (plane & 1) * 80, 80), 80)

        def place(target):
            for head in range(GROUP):
                target[rows, head * HD : head * HD + HD] = ref[first + head * 80 : first + head * 80 + 80]

        pl.when(((plane >> 1) & 1) == ci[0])(lambda: place(keep_w_ref))
        pl.when(((plane >> 1) & 1) != ci[0])(lambda: place(give_w_ref))
    refs = (g0, g1, g2, g3)
    levels = []
    for x in range(NX):
        parts = refs[x][256:272].astype(F32)
        levels.append(parts[0:1] + parts[1:2] + parts[2:3])
    top = jnp.maximum(jnp.maximum(levels[0], levels[1]), jnp.maximum(levels[2], levels[3]))
    shares = [jnp.exp(level - top) for level in levels]
    total = shares[0] + shares[1] + shares[2] + shares[3]
    shared = jnp.zeros((128, 512), F32)
    for x in range(NX):
        head = (xi[0] + x) & (NX - 1)
        a_ref[pl.ds(pl.multiple_of(head * 128, 128), 128)] = refs[x][0:128]
        shared = shared + refs[x][128:256].astype(F32) * (shares[x] / total)
    a_ref[512:640] = shared.astype(BF)
    multiply(give_w_ref, a_ref, give_ref)


def hand_on_kernel(below_w, above_w, attended, below_ref, above_ref):
    del below_w, above_w, attended, below_ref, above_ref


def multiply(w_ref, a_ref, out_ref):
    for y in range(4):
        part = dot(w_ref[y * 160 : y * 160 + 160], a_ref[...], (1, 0)).astype(BF)
        for x in range(NX):
            out_ref[x * 4 + y] = part[:, x * 128 : x * 128 + 128]


def keep_kernel(a_ref, w_ref, out_ref):
    multiply(w_ref, a_ref, out_ref)


def final_kernel(r_ref, out_ref, t_ref):
    for x in range(NX):
        total = r_ref[x * 4].astype(F32)
        for y in range(1, 4):
            total = total + r_ref[x * 4 + y].astype(F32)
        t_ref[x * 80 : x * 80 + 80] = total[0:80]
        t_ref[320 + x * 80 : 320 + x * 80 + 80] = total[80:160]
    out_ref[...] = t_ref[...].T.astype(BF)


def call(kernel, out, specs, out_specs=VMEM, scratch=(), limit=LIMIT, aliases=None):
    return pl.pallas_call(
        kernel,
        out_shape=out,
        in_specs=specs,
        out_specs=out_specs,
        scratch_shapes=list(scratch),
        input_output_aliases=aliases or {},
        compiler_params=pltpu.CompilerParams(vmem_limit_bytes=limit),
    )


def shape(*dims):
    return jax.ShapeDtypeStruct(dims, BF)


def from_plane(value, step):
    return lax.ppermute(value, "z", [((i + step) % NZ, i) for i in range(NZ)])


def from_either(value, step):
    pairs = [((z + (step, -step)[core]) % NZ * 2 + core, z * 2 + core) for z in range(NZ) for core in range(2)]
    return lax.ppermute(value, ("z", "c"), pairs)


def per_device(query_input, key_input, value_input, query_gain, key_gain, band_lists, out_weight):
    plane = ("x", "y", "c")
    lists = band_lists.reshape(-1)
    zi = lax.axis_index("z").reshape(1)
    xi = lax.axis_index("x").reshape(1)
    packed = call(
        pack_kernel,
        shape(32, CHUNK, HD),
        [ANY] * 5,
        ANY,
        [
            pltpu.VMEM((QROWS, D), BF),
            pltpu.VMEM((HALF, D), BF),
            pltpu.VMEM((HALF, D), BF),
            pltpu.VMEM((1, D), F32),
            pltpu.VMEM((1, D), F32),
            pltpu.VMEM((32, CHUNK, HD), BF),
            pltpu.SemaphoreType.DMA((5,)),
            pltpu.SemaphoreType.DMA((NX,)),
        ],
        ALL,
    )(query_input, key_input, value_input, query_gain.reshape(1, -1), key_gain.reshape(1, -1))
    packed, columns = lax.optimization_barrier((packed, out_weight))
    columns = columns.reshape(GROUP, HD, 80).transpose(0, 2, 1).reshape(BLOCK, HD)
    held = [columns] + [from_either(columns, step) for step in HELD[1:]]
    last = from_either(columns, LAST)
    mine = lax.all_to_all(packed, plane, split_axis=0, concat_axis=0, tiled=True)
    up, down = call(select_kernel, (shape(SENT, HD),) * 2, [SMEM, SMEM, VMEM], (VMEM, VMEM))(lists, zi, mine)
    before = lax.ppermute(up, "z", [(i, i + 1) for i in range(NZ - 1)])
    after = lax.ppermute(down, "z", [(i + 1, i) for i in range(NZ - 1)])
    sums, stats = call(
        attend_own_kernel,
        (jax.ShapeDtypeStruct((256, 512), F32), jax.ShapeDtypeStruct((8, 512), F32)),
        [SMEM, SMEM, VMEM],
        (VMEM, VMEM),
        [pltpu.VMEM((1024, HD), BF), pltpu.VMEM((1024, HD), BF), pltpu.VMEM((256, HD), BF), pltpu.VMEM((256, HD), BF)],
    )(lists, zi, mine)
    joined = call(join_kernel, shape(3 * BLOCK, HD), [VMEM] * 3 + [ANY] * 2)(*held, last, stats)
    attended = call(attend_rest_kernel, shape(304, 512), [SMEM, SMEM] + [VMEM] * 5)(
        lists, zi, mine, before, after, sums, stats
    )
    above_w, below_w = from_plane(joined, 1), from_plane(joined, -1)
    below_again, above_again = call(
        hand_on_kernel, (shape(3 * BLOCK, HD),) * 2, [ANY] * 3, (ANY, ANY), aliases={0: 0, 1: 1}
    )(below_w, above_w, attended)
    below2, above2 = from_plane(below_again, -1), from_plane(above_again, 1)
    gathered = [attended] + [
        lax.ppermute(attended, "x", [((i + step) % NX, i) for i in range(NX)]) for step in (1, 2, 3)
    ]
    ci = lax.axis_index("c").reshape(1)
    give, a, keep_w = call(
        project_kernel,
        (shape(16, 160, 128), shape(640, 512), shape(640, 640)),
        [SMEM, SMEM, SMEM] + [VMEM] * 12,
        (VMEM, VMEM, VMEM),
        [pltpu.VMEM((640, 640), BF)],
    )(ci, zi, xi, *gathered, *held, last, below_again, above_again, below2, above2)
    other = lax.ppermute(give, "c", [(0, 1), (1, 0)])
    keep = call(keep_kernel, shape(16, 160, 128), [VMEM, VMEM])(a, keep_w)
    terms = (keep.astype(F32) + other.astype(F32)).astype(BF)
    summands = lax.all_to_all(terms, ("x", "y"), split_axis=0, concat_axis=0, tiled=True)
    return call(final_kernel, shape(128, 640), [VMEM], VMEM, [pltpu.VMEM((640, 128), F32)])(summands)


def solution(mesh):
    split = Mesh(mesh.devices.reshape(NZ, NX, 4, 2), ("z", "x", "y", "c"))
    rows = P(("z", "x", "y", "c"), None)
    return jax.shard_map(
        per_device,
        mesh=split,
        in_specs=(rows, rows, rows, P(), P(), P(), P(("y", "c"), ("z", "x"))),
        out_specs=P(("z", "x"), ("y", "c")),
        check_vma=False,
    )
```
